256 devices in a mesh: segment: 2 (over core), expert: 32 (over y, z), tensor: 4 (over x).
Axes of the slice: x: 4, y: 4, z: 8, core: 2. Of those that a mesh axis runs over, the one named last changes fastest.
Arguments:
- activations: bfloat16 [2, 2048, 2560], P('segment', 'expert', 'tensor'), may hold values from -48 to 48
- expert_ids: int32 [2, 2048, 6], P(None, 'expert'), may hold values from 0 to 63, as said below
- route_weights: float32 [2, 2048, 6], P(None, 'expert'), may hold values from 0.05 to 1
- gain_dense: float32 [2560], replicated, may hold values from 0.25 to 1.75
- gain_expert: float32 [2560], replicated, may hold values from 0.25 to 1.75
- dense_gate: bfloat16 [2560, 6144], P('expert', 'tensor'), may hold values from -0.125 to 0.125
- dense_up: bfloat16 [2560, 6144], P('expert', 'tensor'), may hold values from -0.125 to 0.125
- dense_down: bfloat16 [2560, 6144], P('expert', 'tensor'), may hold values from -0.078125 to 0.078125
- expert_gate: bfloat16 [64, 2560, 1536], P('expert', None, 'tensor'), may hold values from -0.125 to 0.125
- expert_up: bfloat16 [64, 2560, 1536], P('expert', None, 'tensor'), may hold values from -0.125 to 0.125
- expert_down: bfloat16 [64, 1536, 2560], P('expert', 'tensor'), may hold values from -0.15625 to 0.15625
Outputs:
- sections: bfloat16 [2, 2, 2048, 2560], P('segment', None, 'expert', 'tensor')
The draws below stay inside these ranges and needn't reach their ends.
Inputs may be any that keep to these rules, and one draw needn't show every extreme that they name: `expert_ids`: each token names 6 different experts. Split each micro-batch's tokens into blocks of 64 in order: no expert is named by more than 12 tokens of one block, and in every micro-batch one expert is named by exactly 12 tokens of every block.
All inputs are finite; a program needn't handle non-finite values.
Results may differ from the reference program's by a relative error of at most 0.009.
Values may be sent and summed in bfloat16 or wider, within the bound.
A program may use at most 128 MiB of HBM per device.

```python
import math
import jax
import jax.numpy as jnp
from jax import lax

D = 2560
FF = 6144
H = 1536
TOP = 6
MICRO = 2
TOK_DEV = 64
EXPERTS = 64
TOKENS = 2048
CAP = 12
N_EXPERT = 32
N_TENSOR = 4


def draw_activations(key, part):
    key_cols, key_rows, key_values = jax.random.split(jax.random.fold_in(key, 11), 3)
    position = jnp.arange(D, dtype=jnp.float32) / D
    row_scale = jnp.exp(jax.random.uniform(key_rows, (MICRO, TOKENS, 1), jnp.float32, -0.8, 0.8))
    trend = 2.3 * (position - 0.5)
    column_scale = jnp.exp(trend + jax.random.uniform(key_cols, (D,), jnp.float32, -0.4, 0.4))
    values = jax.random.truncated_normal(key_values, -4.0, 4.0, (MICRO, TOKENS, D), jnp.float32)
    return (values * column_scale * row_scale).astype(jnp.bfloat16)


def draw_expert_ids(key, part):
    blocks = TOKENS // TOK_DEV
    hot_experts = jax.random.randint(jax.random.fold_in(key, 21), (MICRO,), 0, EXPERTS)
    block_keys = jax.random.split(jax.random.fold_in(key, 22), MICRO * blocks)
    block_keys = block_keys.reshape((MICRO, blocks) + block_keys.shape[1:])

    def one_block(block_key, hot_expert):
        key_pick, key_order, key_within = jax.random.split(block_key, 3)
        others = jnp.arange(EXPERTS - 1, dtype=jnp.int32)
        others = others + (others >= hot_expert).astype(jnp.int32)
        tickets = jnp.repeat(others, CAP)
        chosen = tickets[jax.random.permutation(key_pick, tickets.shape[0])[:TOK_DEV * TOP - CAP]]
        labels = jnp.sort(jnp.concatenate([jnp.full((CAP,), hot_expert, jnp.int32), chosen]))
        dealt_rows = labels.reshape(TOP, TOK_DEV).T
        dealt_rows = dealt_rows[jax.random.permutation(key_order, TOK_DEV)]
        orders = jax.vmap(lambda row_key: jax.random.permutation(row_key, TOP))(jax.random.split(key_within, TOK_DEV))
        return jnp.take_along_axis(dealt_rows, orders, axis=1)
    drawn_ids = jax.vmap(jax.vmap(one_block, in_axes=(0, None)), in_axes=(0, 0))(block_keys, hot_experts)
    return drawn_ids.reshape(MICRO, TOKENS, TOP).astype(jnp.int32)


def block_scale(key, extent, cuts, smallest, largest):
    def one(axis_at, blocks):
        heights = jax.random.uniform(jax.random.fold_in(jax.random.fold_in(key, 6), axis_at), (blocks,), jnp.float32, smallest / len(cuts), largest / len(cuts))
        return jnp.repeat(jnp.exp(heights), extent[axis_at] // blocks).reshape((-1,) + (1,) * (len(extent) - axis_at - 1))

    gain = one(*cuts[0])
    for cut in cuts[1:]:
        gain = gain * one(*cut)
    return gain


def noise(stream_key, extent, deviation, reach, cuts=(), kind=jnp.bfloat16):
    drawn = jax.random.normal(stream_key, extent, jnp.float32) * deviation
    if len(cuts) > 0:
        drawn = block_scale(stream_key, extent, cuts, -0.22, 0.18) * drawn
    return jnp.clip(drawn, min=-reach, max=reach).astype(kind)


def setup_inputs(seed: int = 0) -> dict:
    arg_keys = jax.random.split(jax.random.key(seed), 12)
    return {
        "activations": draw_activations(jax.random.fold_in(arg_keys[11], 71), 0),
        "expert_ids": draw_expert_ids(jax.random.fold_in(arg_keys[11], 71), 0),
        "route_weights": jnp.clip(jnp.exp(math.log(1.0) - 2.9957323 * jax.random.uniform(arg_keys[2], (MICRO, TOKENS, TOP), jnp.float32) ** block_scale(arg_keys[2], (MICRO, TOKENS, TOP), ((1, 32),), -0.2, 0.2)), 0.05, 1.0),
        "gain_dense": jnp.clip(1.0 + 0.15 * jax.random.normal(arg_keys[3], (D,), jnp.float32), 0.25, 1.75),
        "gain_expert": jnp.clip(1.0 + 0.15 * jax.random.normal(arg_keys[4], (D,), jnp.float32), 0.25, 1.75),
        "dense_gate": noise(arg_keys[5], (D, FF), D ** -0.5, 0.125, ((0, 32), (1, 4))),
        "dense_up": noise(arg_keys[6], (D, FF), D ** -0.5, 0.125, ((0, 32), (1, 4))),
        "dense_down": noise(arg_keys[7], (D, FF), FF ** -0.5, 0.078125, ((0, 32), (1, 4))),
        "expert_gate": noise(arg_keys[8], (EXPERTS, D, H), D ** -0.5, 0.125, ((0, 32), (2, 4))),
        "expert_up": noise(arg_keys[9], (EXPERTS, D, H), D ** -0.5, 0.125, ((0, 32), (2, 4))),
        "expert_down": noise(arg_keys[10], (EXPERTS, H, D), H ** -0.5, 0.15625, ((0, 32), (1, 4))),
    }


EPSILON = 1e-06

def normalize(values, gain_row):
    inverse = lax.rsqrt(lax.optimization_barrier(jnp.mean(values * values, axis=-1, keepdims=True)) + EPSILON)
    return values * inverse * gain_row

def mixture(normed, expert_ids_block, route_block, expert_gate, expert_up, expert_down):
    flat_ids = expert_ids_block.reshape(-1)
    picks_total = flat_ids.shape[0]
    blocks = jnp.arange(picks_total, dtype=jnp.int32) // (TOK_DEV * TOP)
    one_hot = (flat_ids[:, None] == jnp.arange(EXPERTS, dtype=jnp.int32)[None, :]).astype(jnp.int32)
    running = jnp.cumsum(one_hot.reshape(N_EXPERT, TOK_DEV * TOP, EXPERTS), axis=1).reshape(picks_total, EXPERTS)
    ranks = lax.optimization_barrier(jnp.sum((running - 1) * one_hot, axis=1))
    slots = ((flat_ids * N_EXPERT + blocks) * CAP + ranks).astype(jnp.int32)
    owners = jnp.arange(picks_total, dtype=jnp.int32) // TOP
    rows_per_expert = N_EXPERT * CAP
    sources = jnp.full((EXPERTS * rows_per_expert,), TOKENS, jnp.int32).at[slots].set(owners)
    shares = jnp.zeros((EXPERTS * rows_per_expert,), jnp.float32).at[slots].set(route_block.reshape(-1))
    padded = jnp.concatenate([normed, jnp.zeros((1, D), normed.dtype)], axis=0)
    hidden_part = H // N_TENSOR

    def one_expert(totals, inputs):
        gate_weight, up_weight, down_weight, source_rows, share_rows = inputs
        values = padded[source_rows]
        gate_sums = jnp.dot(values, gate_weight, preferred_element_type=jnp.float32)
        upward = jnp.dot(values, up_weight, preferred_element_type=jnp.float32)
        hidden = (jax.nn.silu(gate_sums) * upward).astype(jnp.bfloat16)
        output = jnp.zeros((rows_per_expert, D), jnp.float32)
        for block_index in range(N_TENSOR):
            first_unit = block_index * hidden_part
            piece_sum = jnp.dot(hidden[:, first_unit:first_unit + hidden_part], down_weight[first_unit:first_unit + hidden_part], preferred_element_type=jnp.float32).astype(jnp.bfloat16)
            output = output + lax.optimization_barrier(piece_sum).astype(jnp.float32)
        rounded = lax.optimization_barrier(output.astype(jnp.bfloat16)).astype(jnp.float32)
        totals = totals.at[source_rows].add(share_rows[:, None] * rounded)
        return (totals, None)
    totals, unused = lax.scan(one_expert, jnp.zeros((TOKENS + 1, D), jnp.float32), (expert_gate, expert_up, expert_down, sources.reshape(EXPERTS, rows_per_expert), shares.reshape(EXPERTS, rows_per_expert)))
    return totals[:TOKENS]

def reference(activations, expert_ids, route_weights, gain_dense, gain_expert, dense_gate, dense_up, dense_down, expert_gate, expert_up, expert_down):
    firsts = []
    seconds = []
    for micro_index in range(MICRO):
        inputs = activations[micro_index].astype(jnp.float32)
        normed = normalize(inputs, gain_dense).astype(jnp.bfloat16)
        gate_sums = jnp.dot(normed, dense_gate, preferred_element_type=jnp.float32)
        upward = jnp.dot(normed, dense_up, preferred_element_type=jnp.float32)
        hidden = (jax.nn.silu(gate_sums) * upward).astype(jnp.bfloat16)
        projected = lax.dot_general(hidden, dense_down, (((1,), (1,)), ((), ())), preferred_element_type=jnp.float32)
        middle = (inputs + projected).astype(jnp.bfloat16)
        middle_wide = middle.astype(jnp.float32)
        expert_in = normalize(middle_wide, gain_expert).astype(jnp.bfloat16)
        mixed = mixture(expert_in, expert_ids[micro_index], route_weights[micro_index], expert_gate, expert_up, expert_down)
        firsts.append(middle)
        seconds.append((middle_wide + mixed).astype(jnp.bfloat16))
    return jnp.stack([jnp.stack(firsts), jnp.stack(seconds)])
```

```python
import functools

import jax
import jax.numpy as jnp
from jax import lax
from jax.experimental import pallas as pl
from jax.experimental.pallas import tpu as pltpu
from jax.sharding import PartitionSpec as P

EPSILON = 1e-06
MESH = pl.DeviceIdType.MESH
CAP = 12
SPLIT = (4, 8)


def wait_bytes(ref, sem):
    pltpu.make_async_copy(ref, ref, sem).wait()


def places(split, tensors):
    ny, nz = split
    c, p, t = lax.axis_index("segment"), lax.axis_index("expert"), lax.axis_index("tensor")
    y, z = p // nz, p % nz

    def device(dc=0, dy=0, dz=0, dt=0):
        return (
            lax.rem(c + dc, 2),
            lax.rem(y + dy + ny, ny) * nz + lax.rem(z + dz + nz, nz),
            lax.rem(t + dt, tensors),
        )

    return c, p, t, y, z, device


def greet(offsets, device):
    barrier = pltpu.get_barrier_semaphore()
    for offset in offsets:
        pl.semaphore_signal(barrier, inc=1, device_id=device(*offset), device_id_type=MESH)
    pl.semaphore_wait(barrier, len(offsets))


def silu(v):
    return v / (1.0 + jnp.exp(-v))


def dense_kernel(
    split,
    tensors,
    x_ref,
    gain_ref,
    gate_ref,
    up_ref,
    down_ref,
    out_ref,
    xbuf,
    nbuf,
    wbuf,
    part,
    prec,
    tok_s,
    tok_r,
    w1_s,
    w1_r,
    ring_s,
    ring_r,
    sib_s,
    sib_r,
    out_s,
    out_r,
):
    ny, nz = split
    half = ny // 2
    c, p, t, y, z, device = places(split, tensors)
    tokens, quarter = x_ref.shape
    rows, width = wbuf.shape[2:]
    per_quarter = quarter // rows
    weights = (gate_ref, up_ref, down_ref)

    group = [(dy, dt) for dt in range(tensors) for dy in range(ny) if dy or dt]
    offsets = {(0, dy, 0, dt) for dy, dt in group} | {(1, 0, 0, 0)}
    offsets |= {(0, 0, 1, 0), (0, 0, nz - 1, 0)}
    greet(sorted(offsets), device)

    def first_hop():
        copies = []
        for dy in range(1, ny):
            there = lax.rem(y + dy, ny)
            for m in range(3):
                columns = pl.ds(pl.multiple_of(there * width, 128), width)
                copies.append(
                    pltpu.make_async_remote_copy(
                        src_ref=weights[m].at[:, columns],
                        dst_ref=wbuf.at[p, m],
                        send_sem=w1_s.at[dy - 1, m],
                        recv_sem=w1_r.at[lax.rem(y, half), m],
                        device_id=device(0, dy, 0, 0),
                        device_id_type=MESH,
                    )
                )
        return copies

    sends_weights = y // half == c

    @pl.when(sends_weights)
    def _():
        for copy in first_hop():
            copy.start()
        for m in range(3):
            columns = pl.ds(pl.multiple_of(y * width, 128), width)
            pltpu.make_async_copy(
                weights[m].at[:, columns], wbuf.at[p, m], w1_r.at[lax.rem(y, half), m]
            ).start()

    token_copies = []
    for i, (dy, dt) in enumerate(group):
        token_copies.append(
            pltpu.make_async_remote_copy(
                src_ref=x_ref,
                dst_ref=xbuf.at[t, y],
                send_sem=tok_s.at[i],
                recv_sem=tok_r.at[i],
                device_id=device(0, dy, 0, dt),
                device_id_type=MESH,
            )
        )
        token_copies[-1].start()
    xbuf[t, y] = x_ref[...]

    right, left = 0, 1
    hops = {}
    for a in range(half):
        far, near = nz // 2, (nz - 1) // 2
        hops[right, a], hops[left, a] = (far, near) if a % 2 == 0 else (near, far)
    started = []

    def piece(a, dz):
        return (half * c + a) * nz + lax.rem(z + dz + nz, nz)

    def forward(direction, a, step):
        sign = 1 if direction == right else -1
        at = piece(a, -sign * (step - 1))
        copy = pltpu.make_async_remote_copy(
            src_ref=wbuf.at[at],
            dst_ref=wbuf.at[at],
            send_sem=ring_s.at[direction, a, step - 1],
            recv_sem=ring_r.at[direction, a, step - 1],
            device_id=device(0, 0, sign if sign > 0 else nz - 1, 0),
            device_id_type=MESH,
        )
        copy.start()
        started.append(copy)

    def share(a, dz):
        at = piece(a, dz)
        copy = pltpu.make_async_remote_copy(
            src_ref=wbuf.at[at],
            dst_ref=wbuf.at[at],
            send_sem=sib_s.at[a, dz % nz],
            recv_sem=sib_r.at[a, dz % nz],
            device_id=device(1, 0, 0, 0),
            device_id_type=MESH,
        )
        copy.start()
        started.append(copy)

    for a in range(half):
        for m in range(3):
            wait_bytes(wbuf.at[piece(a, 0), m], w1_r.at[a, m])
        for direction in (right, left):
            if hops[direction, a] >= 1:
                forward(direction, a, 1)
        share(a, 0)

    for i in range(len(group)):
        wait_bytes(xbuf.at[0, 0], tok_r.at[i])

    def norm_block(j, carry):
        squares = jnp.zeros((tokens, 1), jnp.float32)
        for q in range(tensors):
            values = xbuf[q, j].astype(jnp.float32)
            squares += jnp.sum(values * values, axis=1, keepdims=True)
        inverse = lax.rsqrt(squares / (quarter * tensors) + EPSILON)
        for q in range(tensors):
            values = xbuf[q, j].astype(jnp.float32)
            nbuf[q, j] = (values * inverse * gain_ref[q]).astype(jnp.bfloat16)
        return carry

    for step in range(1, nz // 2 + 1):
        for a in range(half):
            for direction in (right, left):
                if step > hops[direction, a]:
                    continue
                sign = 1 if direction == right else -1
                wait_bytes(wbuf.at[piece(a, -sign * step)], ring_r.at[direction, a, step - 1])
                if step + 1 <= hops[direction, a]:
                    forward(direction, a, step + 1)
                share(a, -sign * step)
        if step == 1:
            lax.fori_loop(0, ny, norm_block, 0)
    for a in range(half):
        for dz in range(nz):
            at = (half * (1 - c) + a) * nz + lax.rem(z + dz, nz)
            wait_bytes(wbuf.at[at], sib_r.at[a, dz])

    gate_sums = jnp.zeros((ny * tokens, width), jnp.float32)
    upward = jnp.zeros((ny * tokens, width), jnp.float32)
    for q in range(tensors):
        normed = nbuf[q].reshape(ny * tokens, quarter)
        held = pl.ds(q * per_quarter, per_quarter)
        gate_sums += jnp.dot(
            normed, wbuf[held, 0].reshape(quarter, width), preferred_element_type=jnp.float32
        )
        upward += jnp.dot(
            normed, wbuf[held, 1].reshape(quarter, width), preferred_element_type=jnp.float32
        )
    hidden = (silu(gate_sums) * upward).astype(jnp.bfloat16)

    order = [dt for dt in range(tensors) if dt] + [0]
    for dt in order:
        there = lax.rem(t + dt, tensors)
        down = wbuf[pl.ds(there * per_quarter, per_quarter), 2].reshape(quarter, width)
        result = lax.dot_general(
            hidden, down, (((1,), (1,)), ((), ())), preferred_element_type=jnp.float32
        )
        part[dt] = result.astype(jnp.bfloat16).reshape(ny, tokens, quarter)
        for i, (dy, other) in enumerate(group):
            if other != dt:
                continue
            copy = pltpu.make_async_remote_copy(
                src_ref=part.at[dt, lax.rem(y + dy, ny)],
                dst_ref=prec.at[i],
                send_sem=out_s.at[i],
                recv_sem=out_r.at[i],
                device_id=device(0, dy, 0, dt),
                device_id_type=MESH,
            )
            copy.start()
            started.append(copy)
    total = x_ref[...].astype(jnp.float32)
    summed = part[0, y].astype(jnp.float32)
    for i in range(len(group)):
        wait_bytes(prec.at[i], out_r.at[i])
        summed += prec[i].astype(jnp.float32)
    out_ref[...] = (total + summed).astype(jnp.bfloat16)

    for copy in token_copies + started:
        copy.wait_send()

    @pl.when(sends_weights)
    def _():
        for copy in first_hop():
            copy.wait_send()


def dense_section(x, gain, gate, up, down, split, tensors):
    ny, nz = split
    half = ny // 2
    tokens, quarter = x.shape
    rows, hidden = gate.shape
    width = hidden // ny
    group = ny * tensors - 1
    dma = pltpu.SemaphoreType.DMA
    vmem = pl.BlockSpec(memory_space=pltpu.VMEM)
    return pl.pallas_call(
        functools.partial(dense_kernel, split, tensors),
        out_shape=jax.ShapeDtypeStruct((tokens, quarter), jnp.bfloat16),
        in_specs=[vmem] * 5,
        out_specs=vmem,
        scratch_shapes=[
            pltpu.VMEM((tensors, ny, tokens, quarter), jnp.bfloat16),
            pltpu.VMEM((tensors, ny, tokens, quarter), jnp.bfloat16),
            pltpu.VMEM((ny * nz, 3, rows, width), jnp.bfloat16),
            pltpu.VMEM((tensors, ny, tokens, quarter), jnp.bfloat16),
            pltpu.VMEM((group, tokens, quarter), jnp.bfloat16),
            dma((group,)),
            dma((group,)),
            dma((ny - 1, 3)),
            dma((half, 3)),
            dma((2, half, nz // 2)),
            dma((2, half, nz // 2)),
            dma((half, nz)),
            dma((half, nz)),
            dma((group,)),
            dma((group,)),
        ],
        compiler_params=pltpu.CompilerParams(
            collective_id=0, has_side_effects=True, vmem_limit_bytes=48 * 2**20
        ),
        name="dense_section",
    )(x, gain, gate, up, down)


def expert_kernel(
    split,
    tensors,
    middle_ref,
    ids_ref,
    route_ref,
    gain_ref,
    gate_hbm,
    up_hbm,
    down_hbm,
    out_ref,
    gate,
    up,
    down,
    mids,
    sums,
    outgoing,
    arrived,
    pieces,
    pieces_in,
    summed,
    returned,
    mixes,
    w_sem,
    mid_s,
    mid_r,
    sum_s,
    sum_r,
    go_s,
    go_r,
    x_s,
    x_r,
    piece_s,
    piece_r,
    back_s,
    back_r,
    mix_s,
    mix_r,
):
    ny, nz = split
    chips = ny * nz
    c, p, t, y, z, device = places(split, tensors)
    tokens, quarter = middle_ref.shape
    slots = 2 * CAP
    all_slots = chips * slots
    hidden_width = gate.shape[1]

    loads = [
        pltpu.make_async_copy(far.at[c], near, w_sem.at[i])
        for i, (far, near) in enumerate(((gate_hbm, gate), (up_hbm, up), (down_hbm, down)))
    ]
    for load in loads:
        load.start()

    offsets = {(0, dy, dz, 0) for dy in range(ny) for dz in range(nz) if dy or dz}
    offsets |= {(dc, 0, 0, dt) for dc in range(2) for dt in range(tensors) if dc or dt}
    greet(sorted(offsets), device)

    own = middle_ref[...]
    mids[c] = own
    wide = own.astype(jnp.float32)
    sums[t, c] = jnp.broadcast_to(jnp.sum(wide * wide, axis=1, keepdims=True), (tokens, 128))
    started = []
    mid_copy = pltpu.make_async_remote_copy(
        src_ref=mids.at[c],
        dst_ref=mids.at[c],
        send_sem=mid_s,
        recv_sem=mid_r,
        device_id=device(1, 0, 0, 0),
        device_id_type=MESH,
    )
    mid_copy.start()
    started.append(mid_copy)
    others = [(dc, dt) for dc in range(2) for dt in range(tensors) if dc or dt]
    for i, (dc, dt) in enumerate(others):
        copy = pltpu.make_async_remote_copy(
            src_ref=sums.at[t, c],
            dst_ref=sums.at[t, c],
            send_sem=sum_s.at[i],
            recv_sem=sum_r.at[i],
            device_id=device(dc, 0, 0, dt),
            device_id_type=MESH,
        )
        copy.start()
        started.append(copy)

    def expert_at(k):
        there = lax.rem(y + k // nz, ny) * nz + lax.rem(z + k % nz, nz)
        return 2 * there + c

    experts = expert_at(lax.broadcasted_iota(jnp.int32, (2 * tokens, chips), 1))
    named = jnp.zeros((2 * tokens, chips), jnp.float32)
    share = jnp.zeros((2 * tokens, chips), jnp.float32)
    for j in range(ids_ref.shape[1]):
        same = ids_ref[:, j : j + 1] == experts
        named += jnp.where(same, 1.0, 0.0)
        share += jnp.where(same, route_ref[:, j : j + 1], 0.0)
    one = lax.broadcasted_iota(jnp.int32, (2 * tokens, 2 * tokens), 0)
    two = lax.broadcasted_iota(jnp.int32, (2 * tokens, 2 * tokens), 1)
    before = jnp.where((two < one) & (two // tokens == one // tokens), 1.0, 0.0)
    ranks = jnp.dot(
        before.astype(jnp.bfloat16), named.astype(jnp.bfloat16), preferred_element_type=jnp.float32
    )
    ranks = jnp.where(named > 0.5, ranks, -1.0).astype(jnp.bfloat16)
    share_high = share.astype(jnp.bfloat16)
    share_low = (share - share_high.astype(jnp.float32)).astype(jnp.bfloat16)

    def chooses(shape, slot_axis):
        slot = lax.broadcasted_iota(jnp.int32, shape, slot_axis)
        other = lax.broadcasted_iota(jnp.int32, shape, 1 - slot_axis)
        return slot, other

    slot, chip = chooses((chips, all_slots), 1)
    spread = jnp.where(slot // slots == chip, 1.0, 0.0).astype(jnp.bfloat16)
    slot, chip = chooses((all_slots, chips), 0)
    spread_t = jnp.where(slot // slots == chip, 1.0, 0.0).astype(jnp.bfloat16)

    def is_chosen(found, slot, row):
        rank = (slot % CAP).astype(jnp.float32)
        return (found == rank) & ((slot // CAP) % 2 == row // tokens)

    slot, row = chooses((all_slots, 2 * tokens), 0)
    found = lax.dot_general(
        spread_t, ranks, (((1,), (1,)), ((), ())), preferred_element_type=jnp.float32
    )
    place = jnp.where(is_chosen(found, slot, row), 1.0, 0.0).astype(jnp.bfloat16)

    wait_bytes(mids.at[0], mid_r)
    for i in range(len(others)):
        wait_bytes(sums.at[0, 0], sum_r.at[i])
    normed = []
    for m in range(2):
        squares = sums[0, m]
        for q in range(1, tensors):
            squares += sums[q, m]
        inverse = lax.rsqrt(squares[:, :1] / (quarter * tensors) + EPSILON)
        normed.append(
            (mids[m].astype(jnp.float32) * inverse * gain_ref[t]).astype(jnp.bfloat16)
        )
    normed = jnp.concatenate(normed, axis=0)
    for dy in range(ny):
        rows = place[dy * nz * slots : (dy + 1) * nz * slots]
        block = jnp.dot(rows, normed, preferred_element_type=jnp.float32)
        block = block.reshape(nz, slots, quarter).astype(jnp.bfloat16)
        outgoing[pl.ds(dy * nz, nz)] = block
        if dy == 0:
            arrived[t, 0] = block[0]

        def send(dz, carry, dy=dy):
            k = dy * nz + dz
            pltpu.make_async_remote_copy(
                src_ref=outgoing.at[k],
                dst_ref=arrived.at[t, k],
                send_sem=go_s.at[k],
                recv_sem=go_r.at[k],
                device_id=device(0, dy, dz, 0),
                device_id_type=MESH,
            ).start()
            return carry

        lax.fori_loop(1 if dy == 0 else 0, nz, send, 0)

    for load in loads:
        load.wait()

    def share_chunk(chunk):
        def arrive(dz, carry):
            k = chunk * nz + dz

            @pl.when(k > 0)
            def _():
                wait_bytes(arrived.at[t, k], go_r.at[k])

            return carry

        lax.fori_loop(0, nz, arrive, 0)
        for dt in range(1, tensors):
            held = arrived.at[t, pl.ds(chunk * nz, nz)]
            pltpu.make_async_remote_copy(
                src_ref=held,
                dst_ref=held,
                send_sem=x_s.at[dt - 1, chunk],
                recv_sem=x_r.at[dt - 1, chunk],
                device_id=device(0, 0, 0, dt),
                device_id_type=MESH,
            ).start()

    def compute_chunk(chunk):
        here = pl.ds(chunk * nz, nz)
        for dt in range(1, tensors):
            wait_bytes(arrived.at[0, here], x_r.at[dt - 1, chunk])
        gate_sums = jnp.zeros((nz * slots, hidden_width), jnp.float32)
        upward = jnp.zeros((nz * slots, hidden_width), jnp.float32)
        for q in range(tensors):
            values = arrived[q, here].reshape(nz * slots, quarter)
            some = slice(q * quarter, (q + 1) * quarter)
            gate_sums += jnp.dot(values, gate[some], preferred_element_type=jnp.float32)
            upward += jnp.dot(values, up[some], preferred_element_type=jnp.float32)
        hidden = (silu(gate_sums) * upward).astype(jnp.bfloat16)
        for dt in [*range(1, tensors), 0]:
            there = lax.rem(t + dt, tensors)
            columns = pl.ds(pl.multiple_of(there * quarter, 128), quarter)
            result = jnp.dot(hidden, down[:, columns], preferred_element_type=jnp.float32)
            pieces[dt, here] = result.reshape(nz, slots, quarter).astype(jnp.bfloat16)
            if dt:
                pltpu.make_async_remote_copy(
                    src_ref=pieces.at[dt, here],
                    dst_ref=pieces_in.at[dt - 1, here],
                    send_sem=piece_s.at[dt - 1, chunk],
                    recv_sem=piece_r.at[dt - 1, chunk],
                    device_id=device(0, 0, 0, dt),
                    device_id_type=MESH,
                ).start()

    def return_chunk(chunk):
        here = pl.ds(chunk * nz, nz)
        total = pieces[0, here].astype(jnp.float32)
        for dt in range(1, tensors):
            wait_bytes(pieces_in.at[dt - 1, here], piece_r.at[dt - 1, chunk])
            total += pieces_in[dt - 1, here].astype(jnp.float32)
        summed[here] = total.astype(jnp.bfloat16)

        def give(dz, carry):
            k = chunk * nz + dz

            @pl.when(k > 0)
            def _():
                pltpu.make_async_remote_copy(
                    src_ref=summed.at[k],
                    dst_ref=returned.at[k],
                    send_sem=back_s.at[k],
                    recv_sem=back_r.at[k],
                    device_id=device(0, ny - chunk, nz - dz, 0),
                    device_id_type=MESH,
                ).start()

            return carry

        lax.fori_loop(0, nz, give, 0)

    def stage(i, carry):
        @pl.when(i < ny)
        def _():
            share_chunk(i)

        @pl.when((i >= 1) & (i <= ny))
        def _():
            compute_chunk(i - 1)

        @pl.when(i >= 2)
        def _():
            return_chunk(i - 2)

        return carry

    lax.fori_loop(0, ny + 2, stage, 0)
    returned[0] = summed[0]

    slot, row = chooses((2 * tokens, all_slots), 1)
    row, slot = slot, row
    slot = lax.broadcasted_iota(jnp.int32, (2 * tokens, all_slots), 1)
    row = lax.broadcasted_iota(jnp.int32, (2 * tokens, all_slots), 0)
    found = jnp.dot(ranks, spread, preferred_element_type=jnp.float32)
    chosen = is_chosen(found, slot, row)
    mixers = []
    for part in (share_high, share_low):
        values = jnp.dot(part, spread, preferred_element_type=jnp.float32)
        mixers.append(jnp.where(chosen, values, 0.0).astype(jnp.bfloat16))

    def arrive_back(k, carry):
        wait_bytes(returned.at[k], back_r.at[k])
        return carry

    lax.fori_loop(1, chips, arrive_back, 0)
    back = returned[...].reshape(all_slots, quarter)
    mixed = jnp.dot(mixers[0], back, preferred_element_type=jnp.float32)
    mixed += jnp.dot(mixers[1], back, preferred_element_type=jnp.float32)
    mixes[0] = mixed
    mix_copy = pltpu.make_async_remote_copy(
        src_ref=mixes.at[0],
        dst_ref=mixes.at[1],
        send_sem=mix_s,
        recv_sem=mix_r,
        device_id=device(1, 0, 0, 0),
        device_id_type=MESH,
    )
    mix_copy.start()
    mix_copy.wait_recv()
    both = mixes[0] + mixes[1]
    for m in range(2):
        first = mids[m]
        final = first.astype(jnp.float32) + both[m * tokens : (m + 1) * tokens]
        out_ref[m] = jnp.where(c == 0, first, final.astype(jnp.bfloat16))

    mix_copy.wait_send()
    for copy in started:
        copy.wait_send()

    def sent(k, carry):
        wait_bytes(outgoing.at[k], go_s.at[k])
        wait_bytes(summed.at[k], back_s.at[k])
        return carry

    lax.fori_loop(1, chips, sent, 0)

    def sent_chunk(chunk, carry):
        here = pl.ds(chunk * nz, nz)
        for dt in range(1, tensors):
            wait_bytes(arrived.at[t, here], x_s.at[dt - 1, chunk])
            wait_bytes(pieces.at[dt, here], piece_s.at[dt - 1, chunk])
        return carry

    lax.fori_loop(0, ny, sent_chunk, 0)


def expert_section(middle, ids, route, gain, gate, up, down, split, tensors):
    ny, nz = split
    chips = ny * nz
    tokens, quarter = middle.shape
    slots = 2 * CAP
    hidden = gate.shape[2]
    full = quarter * tensors
    dma = pltpu.SemaphoreType.DMA
    vmem = pl.BlockSpec(memory_space=pltpu.VMEM)
    hbm = pl.BlockSpec(memory_space=pl.ANY)
    rows = (chips, slots, quarter)
    return pl.pallas_call(
        functools.partial(expert_kernel, split, tensors),
        out_shape=jax.ShapeDtypeStruct((2, tokens, quarter), jnp.bfloat16),
        in_specs=[vmem] * 4 + [hbm] * 3,
        out_specs=vmem,
        scratch_shapes=[
            pltpu.VMEM((full, hidden), jnp.bfloat16),
            pltpu.VMEM((full, hidden), jnp.bfloat16),
            pltpu.VMEM((hidden, full), jnp.bfloat16),
            pltpu.VMEM((2, tokens, quarter), jnp.bfloat16),
            pltpu.VMEM((tensors, 2, tokens, 128), jnp.float32),
            pltpu.VMEM(rows, jnp.bfloat16),
            pltpu.VMEM((tensors, *rows), jnp.bfloat16),
            pltpu.VMEM((tensors, *rows), jnp.bfloat16),
            pltpu.VMEM((tensors - 1, *rows), jnp.bfloat16),
            pltpu.VMEM(rows, jnp.bfloat16),
            pltpu.VMEM(rows, jnp.bfloat16),
            pltpu.VMEM((2, 2 * tokens, quarter), jnp.float32),
            dma((3,)),
            dma(()),
            dma(()),
            dma((2 * tensors - 1,)),
            dma((2 * tensors - 1,)),
            dma((chips,)),
            dma((chips,)),
            dma((tensors - 1, ny)),
            dma((tensors - 1, ny)),
            dma((tensors - 1, ny)),
            dma((tensors - 1, ny)),
            dma((chips,)),
            dma((chips,)),
            dma(()),
            dma(()),
        ],
        compiler_params=pltpu.CompilerParams(
            collective_id=1, has_side_effects=True, vmem_limit_bytes=56 * 2**20
        ),
        name="expert_section",
    )(middle, ids, route, gain, gate, up, down)


def body(
    split,
    tensors,
    activations,
    expert_ids,
    route_weights,
    gain_dense,
    gain_expert,
    dense_gate,
    dense_up,
    dense_down,
    expert_gate,
    expert_up,
    expert_down,
):
    tokens, quarter = activations.shape[1:]
    picks = expert_ids.shape[2]
    middle = dense_section(
        activations[0],
        gain_dense.reshape(tensors, 1, quarter),
        dense_gate,
        dense_up,
        dense_down,
        split,
        tensors,
    )
    sections = expert_section(
        middle,
        expert_ids.reshape(2 * tokens, picks),
        route_weights.reshape(2 * tokens, picks),
        gain_expert.reshape(tensors, 1, quarter),
        expert_gate,
        expert_up,
        expert_down,
        split,
        tensors,
    )
    return sections[None]


def solution(mesh, split=SPLIT):
    placed = (
        P("segment", "expert", "tensor"),
        P(None, "expert", None),
        P(None, "expert", None),
        P(),
        P(),
        P("expert", "tensor"),
        P("expert", "tensor"),
        P("expert", "tensor"),
        P("expert", None, "tensor"),
        P("expert", None, "tensor"),
        P("expert", "tensor", None),
    )
    return jax.shard_map(
        functools.partial(body, split, mesh.shape["tensor"]),
        mesh=mesh,
        in_specs=placed,
        out_specs=P("segment", None, "expert", "tensor"),
        check_vma=False,
    )
```

```python
import functools

import jax
import jax.numpy as jnp
from jax import lax
from jax.experimental import pallas as pl
from jax.experimental.pallas import tpu as pltpu
from jax.sharding import PartitionSpec as P

EPSILON = 1e-06
MESH = pl.DeviceIdType.MESH
CAP = 12
SPLIT = (4, 8)


def wait_bytes(ref, sem):
    pltpu.make_async_copy(ref, ref, sem).wait()


def places(split, tensors):
    ny, nz = split
    c, p, t = lax.axis_index("segment"), lax.axis_index("expert"), lax.axis_index("tensor")
    y, z = p // nz, p % nz

    def device(dc=0, dy=0, dz=0, dt=0):
        return (
            lax.rem(c + dc, 2),
            lax.rem(y + dy + ny, ny) * nz + lax.rem(z + dz + nz, nz),
            lax.rem(t + dt, tensors),
        )

    return c, p, t, y, z, device


def greet(offsets, device):
    barrier = pltpu.get_barrier_semaphore()
    for offset in offsets:
        pl.semaphore_signal(barrier, inc=1, device_id=device(*offset), device_id_type=MESH)
    pl.semaphore_wait(barrier, len(offsets))


def silu(v):
    return v / (1.0 + jnp.exp(-v))


def kernel(
    split,
    tensors,
    x_hbm,
    ids_ref,
    route_ref,
    gain_dense_ref,
    gain_expert_ref,
    dense_gate_hbm,
    dense_up_hbm,
    dense_down_hbm,
    gate_hbm,
    up_hbm,
    down_hbm,
    out_ref,
    x_ref,
    dense_held,
    xbuf,
    wbuf,
    hidden_ref,
    part,
    prec,
    gate,
    up,
    down,
    place,
    mixers,
    mids,
    sums,
    outgoing,
    arrived,
    pieces,
    through,
    beside,
    summed,
    returned,
    mixes,
    load_sem,
    tok_s,
    tok_r,
    w1_s,
    w1_r,
    ring_s,
    ring_r,
    sib_s,
    sib_r,
    out_s,
    out_r,
    mid_s,
    mid_r,
    sum_s,
    sum_r,
    go_s,
    go_r,
    x_s,
    x_r,
    f_s,
    f_r,
    half_s,
    half_r,
    side_s,
    side_r,
    back_s,
    back_r,
    mix_s,
    mix_r,
):
    ny, nz = split
    chips = ny * nz
    half = ny // 2
    c, p, t, y, z, device = places(split, tensors)
    tokens, quarter = x_ref.shape
    full = quarter * tensors
    rows, width = wbuf.shape[2:]
    per_quarter = quarter // rows
    slots = 2 * CAP
    all_slots = chips * slots
    hidden_width = gate.shape[1]
    right, left = 0, 1
    signs = (1, -1)

    dense_loads = [
        pltpu.make_async_copy(far, dense_held.at[m], load_sem.at[m])
        for m, far in enumerate((dense_gate_hbm, dense_up_hbm, dense_down_hbm))
    ]
    dense_loads.append(pltpu.make_async_copy(x_hbm, x_ref, load_sem.at[3]))
    expert_loads = [
        pltpu.make_async_copy(far.at[c], near, load_sem.at[4 + i])
        for i, (far, near) in enumerate(((gate_hbm, gate), (up_hbm, up), (down_hbm, down)))
    ]
    for load in dense_loads + expert_loads:
        load.start()

    group = [(dy, dt) for dt in range(tensors) for dy in range(ny) if dy or dt]
    others = [(dc, dt) for dc in range(2) for dt in range(tensors) if dc or dt]
    offsets = {(0, dy, 0, dt) for dy, dt in group}
    offsets |= {(dc, 0, 0, dt) for dc, dt in others}
    offsets |= {(0, dy, dz, 0) for dy in range(ny) for dz in range(nz) if dy or dz}
    greet(sorted(offsets), device)
    for load in dense_loads:
        load.wait()

    started = []

    def send(src, dst, send_sem, recv_sem, to, keep=True):
        copy = pltpu.make_async_remote_copy(
            src_ref=src,
            dst_ref=dst,
            send_sem=send_sem,
            recv_sem=recv_sem,
            device_id=to,
            device_id_type=MESH,
        )
        copy.start()
        if keep:
            started.append(copy)

    def first_hop(m):
        copies = []
        for dy in range(1, ny):
            there = lax.rem(y + dy, ny)
            columns = pl.ds(pl.multiple_of(there * width, 128), width)
            copies.append(
                pltpu.make_async_remote_copy(
                    src_ref=dense_held.at[m, :, columns],
                    dst_ref=wbuf.at[p, m],
                    send_sem=w1_s.at[dy - 1, m],
                    recv_sem=w1_r.at[lax.rem(y, half), m],
                    device_id=device(0, dy, 0, 0),
                    device_id_type=MESH,
                )
            )
        return copies

    sends_weights = y // half == c

    @pl.when(sends_weights)
    def _():
        for m in range(3):
            for copy in first_hop(m):
                copy.start()
            columns = pl.ds(pl.multiple_of(y * width, 128), width)
            pltpu.make_async_copy(
                dense_held.at[m, :, columns], wbuf.at[p, m], w1_r.at[lax.rem(y, half), m]
            ).start()

    kinds = (pl.ds(0, 2), pl.ds(2, 1))
    hops = {}
    for a in range(half):
        far, near = nz // 2, (nz - 1) // 2
        hops[right, a], hops[left, a] = (far, near) if a % 2 == 0 else (near, far)

    def piece(core, a, dz):
        return (half * core + a) * nz + lax.rem(z + dz + nz, nz)

    def forward(kind, a, direction, step):
        sign = signs[direction]
        held = wbuf.at[piece(c, a, -sign * (step - 1)), kinds[kind]]
        send(
            held,
            held,
            ring_s.at[kind, direction, a, step - 1],
            ring_r.at[kind, direction, a, step - 1],
            device(0, 0, sign % nz, 0),
        )

    def hand_over(kind, a, dz):
        held = wbuf.at[piece(c, a, dz), kinds[kind]]
        send(held, held, sib_s.at[kind, a, dz % nz], sib_r.at[kind, a, dz % nz], device(1, 0, 0, 0))

    def begin(kind, a):
        for m in range(2) if kind == 0 else (2,):
            wait_bytes(wbuf.at[piece(c, a, 0), m], w1_r.at[a, m])
        for direction in (right, left):
            if hops[direction, a] >= 1:
                forward(kind, a, direction, 1)
        hand_over(kind, a, 0)

    def ring(kind, a, step):
        for direction in (right, left):
            if step > hops[direction, a]:
                continue
            sign = signs[direction]
            wait_bytes(
                wbuf.at[piece(c, a, -sign * step), kinds[kind]],
                ring_r.at[kind, direction, a, step - 1],
            )
            if step + 1 <= hops[direction, a]:
                forward(kind, a, direction, step + 1)
            hand_over(kind, a, -sign * step)

    def from_other_core(kind, a):
        for dz in range(nz):
            wait_bytes(wbuf.at[piece(1 - c, a, dz), kinds[kind]], sib_r.at[kind, a, dz])

    for a in range(half):
        begin(0, a)

    for i, (dy, dt) in enumerate(group):
        send(x_ref, xbuf.at[t, y], tok_s.at[i], tok_r.at[i], device(0, dy, 0, dt))
    xbuf[t, y] = x_ref[...]

    def expert_at(k):
        there = lax.rem(y + k // nz, ny) * nz + lax.rem(z + k % nz, nz)
        return 2 * there + c

    def iotas(shape):
        return (lax.broadcasted_iota(jnp.int32, shape, i) for i in range(2))

    def plan_routes():
        experts = expert_at(lax.broadcasted_iota(jnp.int32, (chips, tokens), 0))
        one, two = iotas((tokens, tokens))
        before = jnp.where(one < two, 1.0, 0.0).astype(jnp.bfloat16)
        slot, chip = iotas((all_slots, chips))
        spread_t = jnp.where(slot // slots == chip, 1.0, 0.0).astype(jnp.bfloat16)
        chip, slot = iotas((chips, all_slots))
        spread = jnp.where(slot // slots == chip, 1.0, 0.0).astype(jnp.bfloat16)

        def chosen(found, slot, m):
            rank = jnp.where((slot // CAP) % 2 == m, slot % CAP, 2 * tokens)
            return found == rank.astype(jnp.float32)

        for m in range(2):
            named = jnp.zeros((chips, tokens), jnp.float32)
            share = jnp.zeros((chips, tokens), jnp.float32)
            for j in range(ids_ref.shape[0]):
                same = ids_ref[j, m : m + 1, :] == experts
                named += jnp.where(same, 1.0, 0.0)
                share += jnp.where(same, route_ref[j, m : m + 1, :], 0.0)
            ranks = jnp.dot(
                named.astype(jnp.bfloat16), before, preferred_element_type=jnp.float32
            )
            ranks = jnp.where(named > 0.5, ranks, -1.0)
            found = jnp.dot(
                spread_t, ranks.astype(jnp.bfloat16), preferred_element_type=jnp.float32
            )
            slot, token = iotas((all_slots, tokens))
            place[m] = jnp.where(chosen(found, slot, m), 1.0, 0.0).astype(jnp.bfloat16)
            ranks_t, share_t = ranks.T, share.T
            found = jnp.dot(
                ranks_t.astype(jnp.bfloat16), spread, preferred_element_type=jnp.float32
            )
            token, slot = iotas((tokens, all_slots))
            here = chosen(found, slot, m)
            high = share_t.astype(jnp.bfloat16)
            low = (share_t - high.astype(jnp.float32)).astype(jnp.bfloat16)
            for i, values in enumerate((high, low)):
                values = jnp.dot(values, spread, preferred_element_type=jnp.float32)
                mixers[m, i] = jnp.where(here, values, 0.0).astype(jnp.bfloat16)

    def norm_block(j, carry):
        squares = jnp.zeros((tokens, 1), jnp.float32)
        for q in range(tensors):
            values = xbuf[q, j].astype(jnp.float32)
            squares += jnp.sum(values * values, axis=1, keepdims=True)
        inverse = lax.rsqrt(squares / full + EPSILON)
        for q in range(tensors):
            values = xbuf[q, j].astype(jnp.float32)
            gain = gain_dense_ref[q * quarter : (q + 1) * quarter].reshape(1, quarter)
            xbuf[q, j] = (values * inverse * gain).astype(jnp.bfloat16)
        return carry

    def make_hidden():
        gate_sums = jnp.zeros((ny * tokens, width), jnp.float32)
        upward = jnp.zeros((ny * tokens, width), jnp.float32)
        for q in range(tensors):
            normed = xbuf[q].reshape(ny * tokens, quarter)
            held = pl.ds(q * per_quarter, per_quarter)
            gate_sums += jnp.dot(
                normed, wbuf[held, 0].reshape(quarter, width), preferred_element_type=jnp.float32
            )
            upward += jnp.dot(
                normed, wbuf[held, 1].reshape(quarter, width), preferred_element_type=jnp.float32
            )
        hidden_ref[...] = (silu(gate_sums) * upward).astype(jnp.bfloat16)

    def give_quarter(q):
        held = wbuf[pl.ds(q * per_quarter, per_quarter), 2].reshape(quarter, width)
        result = lax.dot_general(
            hidden_ref[...], held, (((1,), (1,)), ((), ())), preferred_element_type=jnp.float32
        )
        part[q] = result.astype(jnp.bfloat16).reshape(ny, tokens, quarter)
        dt = lax.rem(q - t + tensors, tensors)
        for dy in [*range(1, ny), 0]:

            def go(dy=dy):
                at = dy * tensors + dt
                send(
                    part.at[q, lax.rem(y + dy, ny)],
                    prec.at[at],
                    out_s.at[at],
                    out_r.at[at],
                    device(0, dy, 0, dt),
                    keep=False,
                )

            if dy:
                go()
            else:
                pl.when(dt > 0)(go)

    def quarters(a):
        return [q for q in range(tensors) if (q * per_quarter // nz) % half == a]

    steps = nz // 2
    for step in range(1, steps + 1):
        for a in range(half):
            ring(0, a, step)
        if step == 1:
            plan_routes()
            for i in range(len(group)):
                wait_bytes(xbuf.at[0, 0], tok_r.at[i])
            lax.fori_loop(0, ny, norm_block, 0)
        if step == max(steps - 1, 1):
            begin(1, 0)
        if step == steps and half > 1:
            begin(1, half - 1)
    for step in range(1, steps + 1):
        ring(1, 0, step)
        if step == 1:
            for a in range(half):
                from_other_core(0, a)
            make_hidden()
        if half > 1 and step < steps:
            ring(1, half - 1, step)
    from_other_core(1, 0)
    if half == 1:
        for q in range(tensors):
            give_quarter(q)
    else:
        for q in quarters(0):
            give_quarter(q)
        ring(1, half - 1, steps)
        from_other_core(1, half - 1)
        for q in quarters(half - 1):
            give_quarter(q)

    total = part[t, y].astype(jnp.float32)
    for dy, dt in group:
        wait_bytes(prec.at[dy * tensors + dt], out_r.at[dy * tensors + dt])
        total += prec[dy * tensors + dt].astype(jnp.float32)
    own = (x_ref[...].astype(jnp.float32) + total).astype(jnp.bfloat16)

    mids[c] = own
    wide = own.astype(jnp.float32)
    sums[t, c] = jnp.broadcast_to(jnp.sum(wide * wide, axis=1, keepdims=True), (tokens, 128))
    for i, (dc, dt) in enumerate(others):
        send(sums.at[t, c], sums.at[t, c], sum_s.at[i], sum_r.at[i], device(dc, 0, 0, dt))
    send(mids.at[c], mids.at[c], mid_s, mid_r, device(1, 0, 0, 0))
    wait_bytes(mids.at[0], mid_r)
    for i in range(len(others)):
        wait_bytes(sums.at[0, 0], sum_r.at[i])
    normed = []
    gain = gain_expert_ref[pl.ds(pl.multiple_of(t * quarter, 128), quarter)].reshape(1, quarter)
    for m in range(2):
        squares = sums[0, m]
        for q in range(1, tensors):
            squares += sums[q, m]
        inverse = lax.rsqrt(squares[:, :1] / full + EPSILON)
        normed.append((mids[m].astype(jnp.float32) * inverse * gain).astype(jnp.bfloat16))

    for dy in range(ny):
        these = pl.ds(dy * nz * slots, nz * slots)
        block = jnp.dot(place[0, these], normed[0], preferred_element_type=jnp.float32)
        block += jnp.dot(place[1, these], normed[1], preferred_element_type=jnp.float32)
        block = block.reshape(nz, slots, quarter).astype(jnp.bfloat16)
        outgoing[pl.ds(dy * nz, nz)] = block
        if dy == 0:
            arrived[t, 0] = block[0]

        def go(dz, carry, dy=dy):
            k = dy * nz + dz
            send(
                outgoing.at[k],
                arrived.at[t, k],
                go_s.at[k],
                go_r.at[k],
                device(0, dy, dz, 0),
                keep=False,
            )
            return carry

        lax.fori_loop(1 if dy == 0 else 0, nz, go, 0)

    for load in expert_loads:
        load.wait()

    cut = nz // 2
    ways = ((right, 1), (left, tensors - 1))
    far_away = tensors // 2

    def some(chunk):
        return pl.ds(chunk * nz, nz)

    def half_of(chunk, way):
        return pl.ds(chunk * nz + way * cut, cut)

    def share_chunk(chunk):
        def arrive(dz, carry):
            k = chunk * nz + dz

            @pl.when(k > 0)
            def _():
                wait_bytes(arrived.at[t, k], go_r.at[k])

            return carry

        lax.fori_loop(0, nz, arrive, 0)
        held = arrived.at[t, some(chunk)]
        for way, dt in ways:
            send(held, held, x_s.at[way, chunk], x_r.at[way, chunk], device(0, 0, 0, dt), False)

    def forward_chunk(chunk):
        for way, dt in ways:
            source = lax.rem(t + tensors - dt, tensors)
            wait_bytes(arrived.at[source, some(chunk)], x_r.at[way, chunk])
            held = arrived.at[source, half_of(chunk, way)]
            send(held, held, f_s.at[way, chunk], f_r.at[way, chunk], device(0, 0, 0, dt), False)

    def compute_chunk(chunk):
        here = some(chunk)
        source = lax.rem(t + far_away, tensors)
        for way, dt in ways:
            wait_bytes(arrived.at[source, half_of(chunk, way)], f_r.at[way, chunk])
        gate_sums = jnp.zeros((nz * slots, hidden_width), jnp.float32)
        upward = jnp.zeros((nz * slots, hidden_width), jnp.float32)
        for q in range(tensors):
            values = arrived[q, here].reshape(nz * slots, quarter)
            these = slice(q * quarter, (q + 1) * quarter)
            gate_sums += jnp.dot(values, gate[these], preferred_element_type=jnp.float32)
            upward += jnp.dot(values, up[these], preferred_element_type=jnp.float32)
        hidden = (silu(gate_sums) * upward).astype(jnp.bfloat16)
        for dt in (far_away, 1, tensors - 1, 0):
            there = lax.rem(t + dt, tensors)
            columns = pl.ds(pl.multiple_of(there * quarter, 128), quarter)
            result = jnp.dot(hidden, down[:, columns], preferred_element_type=jnp.float32)
            pieces[dt, here] = result.reshape(nz, slots, quarter).astype(jnp.bfloat16)
            if dt == far_away:
                for way, near in ways:
                    send(
                        pieces.at[dt, half_of(chunk, way)],
                        through.at[way, pl.ds(chunk * cut, cut)],
                        half_s.at[way, chunk],
                        half_r.at[way, chunk],
                        device(0, 0, 0, near),
                        False,
                    )

    def relay_chunk(chunk):
        for way, dt in ways:
            came = pl.ds(chunk * cut, cut)
            wait_bytes(through.at[way, came], half_r.at[way, chunk])
            these = half_of(chunk, way)
            both = pieces[dt, these].astype(jnp.float32) + through[way, came].astype(jnp.float32)
            pieces[dt, these] = both.astype(jnp.bfloat16)
            send(
                pieces.at[dt, some(chunk)],
                beside.at[way, some(chunk)],
                side_s.at[way, chunk],
                side_r.at[way, chunk],
                device(0, 0, 0, dt),
                False,
            )

    def return_chunk(chunk):
        here = some(chunk)
        total = pieces[0, here].astype(jnp.float32)
        for way, dt in ways:
            wait_bytes(beside.at[way, here], side_r.at[way, chunk])
            total += beside[way, here].astype(jnp.float32)
        summed[here] = total.astype(jnp.bfloat16)

        def give(dz, carry):
            k = chunk * nz + dz

            @pl.when(k > 0)
            def _():
                send(
                    summed.at[k],
                    returned.at[k],
                    back_s.at[k],
                    back_r.at[k],
                    device(0, ny - chunk, nz - dz, 0),
                    False,
                )

            return carry

        lax.fori_loop(0, nz, give, 0)

    work = (share_chunk, forward_chunk, compute_chunk, relay_chunk, return_chunk)

    def stage(i, carry):
        for lag, act in enumerate(work):

            @pl.when((i >= lag) & (i < ny + lag))
            def _(lag=lag, act=act):
                act(i - lag)

        return carry

    lax.fori_loop(0, ny + len(work) - 1, stage, 0)
    returned[0] = summed[0]

    def arrive_back(k, carry):
        wait_bytes(returned.at[k], back_r.at[k])
        return carry

    lax.fori_loop(1, chips, arrive_back, 0)
    back = returned[...].reshape(all_slots, quarter)
    for m in range(2):
        mixed = jnp.dot(mixers[m, 0], back, preferred_element_type=jnp.float32)
        mixed += jnp.dot(mixers[m, 1], back, preferred_element_type=jnp.float32)
        mixes[0, m] = mixed
    send(mixes.at[0], mixes.at[1], mix_s, mix_r, device(1, 0, 0, 0))
    wait_bytes(mixes.at[1], mix_r)
    for m in range(2):
        first = mids[m]
        final = first.astype(jnp.float32) + (mixes[0, m] + mixes[1, m])
        out_ref[m] = jnp.where(c == 0, first, final.astype(jnp.bfloat16))

    for copy in started:
        copy.wait_send()
    for dy, dt in group:
        wait_bytes(prec.at[0], out_s.at[dy * tensors + dt])

    @pl.when(sends_weights)
    def _():
        for m in range(3):
            for copy in first_hop(m):
                copy.wait_send()

    def sent(k, carry):
        wait_bytes(outgoing.at[k], go_s.at[k])
        wait_bytes(summed.at[k], back_s.at[k])
        return carry

    lax.fori_loop(1, chips, sent, 0)

    def sent_chunk(chunk, carry):
        for way, dt in ways:
            wait_bytes(arrived.at[0, some(chunk)], x_s.at[way, chunk])
            wait_bytes(arrived.at[0, half_of(chunk, way)], f_s.at[way, chunk])
            wait_bytes(arrived.at[0, half_of(chunk, way)], half_s.at[way, chunk])
            wait_bytes(pieces.at[0, some(chunk)], side_s.at[way, chunk])
        return carry

    lax.fori_loop(0, ny, sent_chunk, 0)


def body(
    split,
    tensors,
    activations,
    expert_ids,
    route_weights,
    gain_dense,
    gain_expert,
    dense_gate,
    dense_up,
    dense_down,
    expert_gate,
    expert_up,
    expert_down,
):
    ny, nz = split
    chips = ny * nz
    half = ny // 2
    tokens, quarter = activations.shape[1:]
    full = quarter * tensors
    rows, dense_hidden = dense_gate.shape
    width = dense_hidden // ny
    slots = 2 * CAP
    hidden = expert_gate.shape[2]
    group = ny * tensors - 1
    steps = nz // 2
    bf16, f32 = jnp.bfloat16, jnp.float32
    dma = pltpu.SemaphoreType.DMA
    vmem = pl.BlockSpec(memory_space=pltpu.VMEM)
    hbm = pl.BlockSpec(memory_space=pl.ANY)
    sent_rows = (chips, slots, quarter)
    sections = pl.pallas_call(
        functools.partial(kernel, split, tensors),
        out_shape=jax.ShapeDtypeStruct((2, tokens, quarter), bf16),
        in_specs=[hbm] + [vmem] * 4 + [hbm] * 6,
        out_specs=vmem,
        scratch_shapes=[
            pltpu.VMEM((tokens, quarter), bf16),
            pltpu.VMEM((3, rows, dense_hidden), bf16),
            pltpu.VMEM((tensors, ny, tokens, quarter), bf16),
            pltpu.VMEM((chips, 3, rows, width), bf16),
            pltpu.VMEM((ny * tokens, width), bf16),
            pltpu.VMEM((tensors, ny, tokens, quarter), bf16),
            pltpu.VMEM((ny * tensors, tokens, quarter), bf16),
            pltpu.VMEM((full, hidden), bf16),
            pltpu.VMEM((full, hidden), bf16),
            pltpu.VMEM((hidden, full), bf16),
            pltpu.VMEM((2, chips * slots, tokens), bf16),
            pltpu.VMEM((2, 2, tokens, chips * slots), bf16),
            pltpu.VMEM((2, tokens, quarter), bf16),
            pltpu.VMEM((tensors, 2, tokens, 128), f32),
            pltpu.VMEM(sent_rows, bf16),
            pltpu.VMEM((tensors, *sent_rows), bf16),
            pltpu.VMEM((tensors, *sent_rows), bf16),
            pltpu.VMEM((2, chips // 2, slots, quarter), bf16),
            pltpu.VMEM((2, *sent_rows), bf16),
            pltpu.VMEM(sent_rows, bf16),
            pltpu.VMEM(sent_rows, bf16),
            pltpu.VMEM((2, 2, tokens, quarter), f32),
            dma((7,)),
            dma((group,)),
            dma((group,)),
            dma((ny - 1, 3)),
            dma((half, 3)),
            dma((2, 2, half, steps)),
            dma((2, 2, half, steps)),
            dma((2, half, nz)),
            dma((2, half, nz)),
            dma((ny * tensors,)),
            dma((ny * tensors,)),
            dma(()),
            dma(()),
            dma((2 * tensors - 1,)),
            dma((2 * tensors - 1,)),
            dma((chips,)),
            dma((chips,)),
            dma((2, ny)),
            dma((2, ny)),
            dma((2, ny)),
            dma((2, ny)),
            dma((2, ny)),
            dma((2, ny)),
            dma((2, ny)),
            dma((2, ny)),
            dma((chips,)),
            dma((chips,)),
            dma(()),
            dma(()),
        ],
        compiler_params=pltpu.CompilerParams(
            collective_id=0, has_side_effects=True, vmem_limit_bytes=58 * 2**20
        ),
        name="sections",
    )(
        activations[0],
        expert_ids.transpose(2, 0, 1),
        route_weights.transpose(2, 0, 1),
        gain_dense,
        gain_expert,
        dense_gate,
        dense_up,
        dense_down,
        expert_gate,
        expert_up,
        expert_down,
    )
    return sections[None]


def solution(mesh, split=SPLIT):
    placed = (
        P("segment", "expert", "tensor"),
        P(None, "expert", None),
        P(None, "expert", None),
        P(),
        P(),
        P("expert", "tensor"),
        P("expert", "tensor"),
        P("expert", "tensor"),
        P("expert", None, "tensor"),
        P("expert", None, "tensor"),
        P("expert", "tensor", None),
    )
    return jax.shard_map(
        functools.partial(body, split, mesh.shape["tensor"]),
        mesh=mesh,
        in_specs=placed,
        out_specs=P("segment", None, "expert", "tensor"),
        check_vma=False,
    )
```

```python
import functools

import jax
import jax.numpy as jnp
from jax import lax
from jax.experimental import pallas as pl
from jax.experimental.pallas import tpu as pltpu
from jax.sharding import PartitionSpec as P

EPSILON = 1e-06
MESH = pl.DeviceIdType.MESH
CAP = 12
CHUNKS = 8
SPLIT = (4, 8)


def wait_bytes(ref, sem):
    pltpu.make_async_copy(ref, ref, sem).wait()


def places(split, tensors):
    ny, nz = split
    c, p, t = lax.axis_index("segment"), lax.axis_index("expert"), lax.axis_index("tensor")
    y, z = p // nz, p % nz

    def device(dc=0, dy=0, dz=0, dt=0):
        return (
            lax.rem(c + dc, 2),
            lax.rem(y + dy + ny, ny) * nz + lax.rem(z + dz + nz, nz),
            lax.rem(t + dt, tensors),
        )

    return c, p, t, y, z, device


def greet(offsets, device):
    barrier = pltpu.get_barrier_semaphore()
    for offset in offsets:
        pl.semaphore_signal(barrier, inc=1, device_id=device(*offset), device_id_type=MESH)
    pl.semaphore_wait(barrier, len(offsets))


def silu(v):
    return v / (1.0 + jnp.exp(-v))


def kernel(
    split,
    tensors,
    x_hbm,
    ids_ref,
    route_ref,
    gain_dense_ref,
    gain_expert_ref,
    dense_gate_hbm,
    dense_up_hbm,
    dense_down_hbm,
    gate_hbm,
    up_hbm,
    down_hbm,
    out_ref,
    x_ref,
    dense_held,
    xbuf,
    wbuf,
    hidden_ref,
    part,
    along_x,
    along_y,
    over_x,
    over_y,
    last_y,
    last_x,
    gate,
    up,
    down,
    place,
    mixers,
    mids,
    sums,
    outgoing,
    arrived,
    pieces,
    through,
    beside,
    summed,
    returned,
    mixes,
    load_sem,
    tok_s,
    tok_r,
    w1_s,
    w1_r,
    ring_s,
    ring_r,
    sib_s,
    sib_r,
    a1_s,
    a1_r,
    b1_s,
    b1_r,
    a2_s,
    a2_r,
    b2_s,
    b2_r,
    mid_s,
    mid_r,
    sum_s,
    sum_r,
    go_s,
    go_r,
    x_s,
    x_r,
    f_s,
    f_r,
    half_s,
    half_r,
    side_s,
    side_r,
    back_s,
    back_r,
    mix_s,
    mix_r,
):
    ny, nz = split
    chips = ny * nz
    half = ny // 2
    c, p, t, y, z, device = places(split, tensors)
    tokens, quarter = x_ref.shape
    full = quarter * tensors
    rows, width = wbuf.shape[2:]
    per_quarter = quarter // rows
    slots = 2 * CAP
    all_slots = chips * slots
    hidden_width = gate.shape[1]
    right, left = 0, 1
    signs = (1, -1)
    first, second = pl.ds(0, tokens // 2), pl.ds(tokens // 2, tokens // 2)

    dense_loads = [
        pltpu.make_async_copy(far, dense_held.at[m], load_sem.at[m])
        for m, far in enumerate((dense_gate_hbm, dense_up_hbm, dense_down_hbm))
    ]
    dense_loads.append(pltpu.make_async_copy(x_hbm, x_ref, load_sem.at[3]))
    expert_loads = [
        pltpu.make_async_copy(far.at[c], near, load_sem.at[4 + i])
        for i, (far, near) in enumerate(((gate_hbm, gate), (up_hbm, up), (down_hbm, down)))
    ]
    for load in dense_loads + expert_loads:
        load.start()

    group = [(dy, dt) for dt in range(tensors) for dy in range(ny) if dy or dt]
    others = [(dc, dt) for dc in range(2) for dt in range(tensors) if dc or dt]
    offsets = {(0, dy, 0, dt) for dy, dt in group}
    offsets |= {(dc, 0, 0, dt) for dc, dt in others}
    offsets |= {(0, dy, dz, 0) for dy in range(ny) for dz in range(nz) if dy or dz}
    greet(sorted(offsets), device)
    for load in dense_loads:
        load.wait()

    started = []

    def send(src, dst, send_sem, recv_sem, to, keep=True):
        copy = pltpu.make_async_remote_copy(
            src_ref=src,
            dst_ref=dst,
            send_sem=send_sem,
            recv_sem=recv_sem,
            device_id=to,
            device_id_type=MESH,
        )
        copy.start()
        if keep:
            started.append(copy)

    def first_hop(m):
        copies = []
        for dy in range(1, ny):
            there = lax.rem(y + dy, ny)
            columns = pl.ds(pl.multiple_of(there * width, 128), width)
            copies.append(
                pltpu.make_async_remote_copy(
                    src_ref=dense_held.at[m, :, columns],
                    dst_ref=wbuf.at[p, m],
                    send_sem=w1_s.at[dy - 1, m],
                    recv_sem=w1_r.at[lax.rem(y, half), m],
                    device_id=device(0, dy, 0, 0),
                    device_id_type=MESH,
                )
            )
        return copies

    sends_weights = y // half == c

    @pl.when(sends_weights)
    def _():
        for m in range(3):
            for copy in first_hop(m):
                copy.start()
            columns = pl.ds(pl.multiple_of(y * width, 128), width)
            pltpu.make_async_copy(
                dense_held.at[m, :, columns], wbuf.at[p, m], w1_r.at[lax.rem(y, half), m]
            ).start()

    kinds = (pl.ds(0, 2), pl.ds(2, 1))
    hops = {}
    for a in range(half):
        far, near = nz // 2, (nz - 1) // 2
        hops[right, a], hops[left, a] = (far, near) if a % 2 == 0 else (near, far)

    def piece(core, a, dz):
        return (half * core + a) * nz + lax.rem(z + dz + nz, nz)

    def forward(kind, a, direction, step):
        sign = signs[direction]
        held = wbuf.at[piece(c, a, -sign * (step - 1)), kinds[kind]]
        send(
            held,
            held,
            ring_s.at[kind, direction, a, step - 1],
            ring_r.at[kind, direction, a, step - 1],
            device(0, 0, sign % nz, 0),
        )

    def hand_over(kind, a, dz):
        held = wbuf.at[piece(c, a, dz), kinds[kind]]
        send(held, held, sib_s.at[kind, a, dz % nz], sib_r.at[kind, a, dz % nz], device(1, 0, 0, 0))

    def begin(kind, a):
        for m in range(2) if kind == 0 else (2,):
            wait_bytes(wbuf.at[piece(c, a, 0), m], w1_r.at[a, m])
        for direction in (right, left):
            if hops[direction, a] >= 1:
                forward(kind, a, direction, 1)
        hand_over(kind, a, 0)

    def ring(kind, a, step):
        for direction in (right, left):
            if step > hops[direction, a]:
                continue
            sign = signs[direction]
            wait_bytes(
                wbuf.at[piece(c, a, -sign * step), kinds[kind]],
                ring_r.at[kind, direction, a, step - 1],
            )
            if step + 1 <= hops[direction, a]:
                forward(kind, a, direction, step + 1)
            hand_over(kind, a, -sign * step)

    def from_other_core(kind, a):
        for dz in range(nz):
            wait_bytes(wbuf.at[piece(1 - c, a, dz), kinds[kind]], sib_r.at[kind, a, dz])

    for a in range(half):
        begin(0, a)

    for i, (dy, dt) in enumerate(group):
        send(x_ref, xbuf.at[t, y], tok_s.at[i], tok_r.at[i], device(0, dy, 0, dt))
    xbuf[t, y] = x_ref[...]

    def expert_at(k):
        there = lax.rem(y + k // nz, ny) * nz + lax.rem(z + k % nz, nz)
        return 2 * there + c

    def iotas(shape):
        return (lax.broadcasted_iota(jnp.int32, shape, i) for i in range(2))

    def plan_routes():
        experts = expert_at(lax.broadcasted_iota(jnp.int32, (chips, tokens), 0))
        one, two = iotas((tokens, tokens))
        before = jnp.where(one < two, 1.0, 0.0).astype(jnp.bfloat16)
        slot, chip = iotas((all_slots, chips))
        spread_t = jnp.where(slot // slots == chip, 1.0, 0.0).astype(jnp.bfloat16)
        chip, slot = iotas((chips, all_slots))
        spread = jnp.where(slot // slots == chip, 1.0, 0.0).astype(jnp.bfloat16)

        def chosen(found, slot, m):
            rank = jnp.where((slot // CAP) % 2 == m, slot % CAP, 2 * tokens)
            return found == rank.astype(jnp.float32)

        for m in range(2):
            named = jnp.zeros((chips, tokens), jnp.float32)
            share = jnp.zeros((chips, tokens), jnp.float32)
            for j in range(ids_ref.shape[0]):
                same = ids_ref[j, m : m + 1, :] == experts
                named += jnp.where(same, 1.0, 0.0)
                share += jnp.where(same, route_ref[j, m : m + 1, :], 0.0)
            ranks = jnp.dot(
                named.astype(jnp.bfloat16), before, preferred_element_type=jnp.float32
            )
            ranks = jnp.where(named > 0.5, ranks, -1.0)
            found = jnp.dot(
                spread_t, ranks.astype(jnp.bfloat16), preferred_element_type=jnp.float32
            )
            slot, token = iotas((all_slots, tokens))
            place[m] = jnp.where(chosen(found, slot, m), 1.0, 0.0).astype(jnp.bfloat16)
            ranks_t, share_t = ranks.T, share.T
            found = jnp.dot(
                ranks_t.astype(jnp.bfloat16), spread, preferred_element_type=jnp.float32
            )
            token, slot = iotas((tokens, all_slots))
            here = chosen(found, slot, m)
            high = share_t.astype(jnp.bfloat16)
            low = (share_t - high.astype(jnp.float32)).astype(jnp.bfloat16)
            for i, values in enumerate((high, low)):
                values = jnp.dot(values, spread, preferred_element_type=jnp.float32)
                mixers[m, i] = jnp.where(here, values, 0.0).astype(jnp.bfloat16)

    def norm_block(j, carry):
        squares = jnp.zeros((tokens, 1), jnp.float32)
        for q in range(tensors):
            values = xbuf[q, j].astype(jnp.float32)
            squares += jnp.sum(values * values, axis=1, keepdims=True)
        inverse = lax.rsqrt(squares / full + EPSILON)
        for q in range(tensors):
            values = xbuf[q, j].astype(jnp.float32)
            gain = gain_dense_ref[q * quarter : (q + 1) * quarter].reshape(1, quarter)
            xbuf[q, j] = (values * inverse * gain).astype(jnp.bfloat16)
        return carry

    acc = [jnp.zeros((ny * tokens, width), jnp.float32) for _ in range(2)]

    def add_quarter(q):
        normed = xbuf[q].reshape(ny * tokens, quarter)
        held = pl.ds(q * per_quarter, per_quarter)
        for i in range(2):
            acc[i] += jnp.dot(
                normed, wbuf[held, i].reshape(quarter, width), preferred_element_type=jnp.float32
            )

    def give_quarter(q):
        held = wbuf[pl.ds(q * per_quarter, per_quarter), 2].reshape(quarter, width)
        result = lax.dot_general(
            hidden_ref[...], held, (((1,), (1,)), ((), ())), preferred_element_type=jnp.float32
        )
        part[q] = result.astype(jnp.bfloat16).reshape(ny, tokens, quarter)
        for dy in range(1, ny):
            send(
                part.at[q, lax.rem(y + dy, ny), second],
                along_y.at[dy - 1, q],
                b1_s.at[dy - 1, q],
                b1_r.at[dy - 1, q],
                device(0, dy, 0, 0),
                keep=False,
            )
        dt = lax.rem(q - t + tensors, tensors)

        @pl.when(dt > 0)
        def _():
            send(
                part.at[q, :, first],
                along_x.at[dt - 1],
                a1_s.at[dt - 1],
                a1_r.at[dt - 1],
                device(0, 0, 0, dt),
                keep=False,
            )

    def quarters(a):
        last = [((q + 1) * per_quarter - 1) // nz % half for q in range(tensors)]
        return [q for q in range(tensors) if last[q] == a]

    steps = nz // 2
    early = max(steps - 1, 1)
    for step in range(1, steps + 1):
        for a in range(half):
            ring(0, a, step)
        if step == early:
            begin(1, 0)
            for i in range(len(group)):
                wait_bytes(xbuf.at[0, 0], tok_r.at[i])
            lax.fori_loop(0, ny, norm_block, 0)
        if step == steps and half > 1:
            begin(1, half - 1)
    left_over = list(range(tensors))
    for step in range(1, steps + 1):
        ring(1, 0, step)
        if half > 1 and step < steps:
            ring(1, half - 1, step)
        if step == 1:
            for a in range(half):
                from_other_core(0, a)
        if step < steps and left_over:
            add_quarter(left_over.pop(0))
    for q in left_over:
        add_quarter(q)
    hidden_ref[...] = (silu(acc[0]) * acc[1]).astype(jnp.bfloat16)
    for a in range(half):
        if a:
            ring(1, a, steps)
        from_other_core(1, a)
        for q in quarters(a):
            give_quarter(q)
    plan_routes()

    total = part[t, :, first].astype(jnp.float32)
    for i in range(tensors - 1):
        wait_bytes(along_x.at[i], a1_r.at[i])
        total += along_x[i].astype(jnp.float32)
    over_x[...] = total.astype(jnp.bfloat16)
    for dy in range(1, ny):
        send(
            over_x.at[lax.rem(y + dy, ny)],
            last_y.at[dy - 1],
            a2_s.at[dy - 1],
            a2_r.at[dy - 1],
            device(0, dy, 0, 0),
        )
    total = part[:, y, second].astype(jnp.float32)
    for dy in range(1, ny):
        for q in range(tensors):
            wait_bytes(along_y.at[dy - 1, q], b1_r.at[dy - 1, q])
        total += along_y[dy - 1].astype(jnp.float32)
    over_y[...] = total.astype(jnp.bfloat16)
    for dt in range(1, tensors):
        send(
            over_y.at[lax.rem(t + dt, tensors)],
            last_x.at[dt - 1],
            b2_s.at[dt - 1],
            b2_r.at[dt - 1],
            device(0, 0, 0, dt),
        )
    upper = over_x[y].astype(jnp.float32)
    for dy in range(1, ny):
        wait_bytes(last_y.at[dy - 1], a2_r.at[dy - 1])
        upper += last_y[dy - 1].astype(jnp.float32)
    lower = over_y[t].astype(jnp.float32)
    for dt in range(1, tensors):
        wait_bytes(last_x.at[dt - 1], b2_r.at[dt - 1])
        lower += last_x[dt - 1].astype(jnp.float32)
    total = jnp.concatenate([upper, lower], axis=0)
    own = (x_ref[...].astype(jnp.float32) + total).astype(jnp.bfloat16)

    mids[c] = own
    wide = own.astype(jnp.float32)
    sums[t, c] = jnp.broadcast_to(jnp.sum(wide * wide, axis=1, keepdims=True), (tokens, 128))
    for i, (dc, dt) in enumerate(others):
        send(sums.at[t, c], sums.at[t, c], sum_s.at[i], sum_r.at[i], device(dc, 0, 0, dt))
    send(mids.at[c], mids.at[c], mid_s, mid_r, device(1, 0, 0, 0))
    wait_bytes(mids.at[0], mid_r)
    for i in range(len(others)):
        wait_bytes(sums.at[0, 0], sum_r.at[i])
    normed = []
    gain = gain_expert_ref[pl.ds(pl.multiple_of(t * quarter, 128), quarter)].reshape(1, quarter)
    for m in range(2):
        squares = sums[0, m]
        for q in range(1, tensors):
            squares += sums[q, m]
        inverse = lax.rsqrt(squares[:, :1] / full + EPSILON)
        normed.append((mids[m].astype(jnp.float32) * inverse * gain).astype(jnp.bfloat16))

    per = chips // CHUNKS
    for chunk in range(CHUNKS):
        these = pl.ds(chunk * per * slots, per * slots)
        block = jnp.dot(place[0, these], normed[0], preferred_element_type=jnp.float32)
        block += jnp.dot(place[1, these], normed[1], preferred_element_type=jnp.float32)
        block = block.reshape(per, slots, quarter).astype(jnp.bfloat16)
        outgoing[pl.ds(chunk * per, per)] = block
        if chunk == 0:
            arrived[t, 0] = block[0]

        def go(k, carry):
            send(
                outgoing.at[k],
                arrived.at[t, k],
                go_s.at[k],
                go_r.at[k],
                device(0, k // nz, k % nz, 0),
                keep=False,
            )
            return carry

        lax.fori_loop(max(chunk * per, 1), (chunk + 1) * per, go, 0)

    for load in expert_loads:
        load.wait()

    cut = per // 2
    ways = ((right, 1), (left, tensors - 1))
    far_away = tensors // 2

    def some(chunk):
        return pl.ds(chunk * per, per)

    def half_of(chunk, way):
        return pl.ds(chunk * per + way * cut, cut)

    def share_chunk(chunk):
        def arrive(i, carry):
            k = chunk * per + i

            @pl.when(k > 0)
            def _():
                wait_bytes(arrived.at[t, k], go_r.at[k])

            return carry

        lax.fori_loop(0, per, arrive, 0)
        held = arrived.at[t, some(chunk)]
        for way, dt in ways:
            send(held, held, x_s.at[way, chunk], x_r.at[way, chunk], device(0, 0, 0, dt), False)

    def forward_chunk(chunk):
        for way, dt in ways:
            source = lax.rem(t + tensors - dt, tensors)
            wait_bytes(arrived.at[source, some(chunk)], x_r.at[way, chunk])
            held = arrived.at[source, half_of(chunk, way)]
            send(held, held, f_s.at[way, chunk], f_r.at[way, chunk], device(0, 0, 0, dt), False)

    def compute_chunk(chunk):
        here = some(chunk)
        source = lax.rem(t + far_away, tensors)
        for way, dt in ways:
            wait_bytes(arrived.at[source, half_of(chunk, way)], f_r.at[way, chunk])
        gate_sums = jnp.zeros((per * slots, hidden_width), jnp.float32)
        upward = jnp.zeros((per * slots, hidden_width), jnp.float32)
        for q in range(tensors):
            values = arrived[q, here].reshape(per * slots, quarter)
            these = slice(q * quarter, (q + 1) * quarter)
            gate_sums += jnp.dot(values, gate[these], preferred_element_type=jnp.float32)
            upward += jnp.dot(values, up[these], preferred_element_type=jnp.float32)
        hidden = (silu(gate_sums) * upward).astype(jnp.bfloat16)
        for dt in (far_away, 1, tensors - 1, 0):
            there = lax.rem(t + dt, tensors)
            columns = pl.ds(pl.multiple_of(there * quarter, 128), quarter)
            result = jnp.dot(hidden, down[:, columns], preferred_element_type=jnp.float32)
            pieces[dt, here] = result.reshape(per, slots, quarter).astype(jnp.bfloat16)
            if dt == far_away:
                for way, near in ways:
                    send(
                        pieces.at[dt, half_of(chunk, way)],
                        through.at[way, pl.ds(chunk * cut, cut)],
                        half_s.at[way, chunk],
                        half_r.at[way, chunk],
                        device(0, 0, 0, near),
                        False,
                    )

    def relay_chunk(chunk):
        for way, dt in ways:
            came = pl.ds(chunk * cut, cut)
            wait_bytes(through.at[way, came], half_r.at[way, chunk])
            these = half_of(chunk, way)
            both = pieces[dt, these].astype(jnp.float32) + through[way, came].astype(jnp.float32)
            pieces[dt, these] = both.astype(jnp.bfloat16)
            send(
                pieces.at[dt, some(chunk)],
                beside.at[way, some(chunk)],
                side_s.at[way, chunk],
                side_r.at[way, chunk],
                device(0, 0, 0, dt),
                False,
            )

    def return_chunk(chunk):
        here = some(chunk)
        total = pieces[0, here].astype(jnp.float32)
        for way, dt in ways:
            wait_bytes(beside.at[way, here], side_r.at[way, chunk])
            total += beside[way, here].astype(jnp.float32)
        summed[here] = total.astype(jnp.bfloat16)

        def give(i, carry):
            k = chunk * per + i

            @pl.when(k > 0)
            def _():
                send(
                    summed.at[k],
                    returned.at[k],
                    back_s.at[k],
                    back_r.at[k],
                    device(0, ny - k // nz, nz - k % nz, 0),
                    False,
                )

            return carry

        lax.fori_loop(0, per, give, 0)

    work = ((0, share_chunk), (1, forward_chunk), (2, compute_chunk), (3, relay_chunk), (4, return_chunk))

    def stage(i, carry):
        for lag, act in work:

            @pl.when((i >= lag) & (i < CHUNKS + lag))
            def _(lag=lag, act=act):
                act(i - lag)

        return carry

    lax.fori_loop(0, CHUNKS + len(work) - 1, stage, 0)
    returned[0] = summed[0]

    def arrive_back(k, carry):
        wait_bytes(returned.at[k], back_r.at[k])
        return carry

    mixed = [jnp.zeros((tokens, quarter), jnp.float32) for _ in range(2)]
    for i in range(2):
        low, high = i * chips // 2, (i + 1) * chips // 2
        lax.fori_loop(max(low, 1), high, arrive_back, 0)
        back = returned[low:high].reshape(all_slots // 2, quarter)
        for m in range(2):
            for j in range(2):
                mixer = mixers[m, j, :, low * slots : high * slots]
                mixed[m] += jnp.dot(mixer, back, preferred_element_type=jnp.float32)
    for m in range(2):
        mixes[0, m] = mixed[m]
    send(mixes.at[0], mixes.at[1], mix_s, mix_r, device(1, 0, 0, 0))
    wait_bytes(mixes.at[1], mix_r)
    for m in range(2):
        middle = mids[m]
        final = middle.astype(jnp.float32) + (mixes[0, m] + mixes[1, m])
        out_ref[m] = jnp.where(c == 0, middle, final.astype(jnp.bfloat16))

    for copy in started:
        copy.wait_send()
    for i in range(tensors - 1):
        wait_bytes(along_x.at[i], a1_s.at[i])
    for dy in range(ny - 1):
        for q in range(tensors):
            wait_bytes(along_y.at[dy, q], b1_s.at[dy, q])

    @pl.when(sends_weights)
    def _():
        for m in range(3):
            for copy in first_hop(m):
                copy.wait_send()

    def sent(k, carry):
        wait_bytes(outgoing.at[k], go_s.at[k])
        wait_bytes(summed.at[k], back_s.at[k])
        return carry

    lax.fori_loop(1, chips, sent, 0)

    def sent_chunk(chunk, carry):
        for way, dt in ways:
            wait_bytes(arrived.at[0, some(chunk)], x_s.at[way, chunk])
            wait_bytes(arrived.at[0, half_of(chunk, way)], f_s.at[way, chunk])
            wait_bytes(arrived.at[0, half_of(chunk, way)], half_s.at[way, chunk])
            wait_bytes(pieces.at[0, some(chunk)], side_s.at[way, chunk])
        return carry

    lax.fori_loop(0, CHUNKS, sent_chunk, 0)


def body(
    split,
    tensors,
    activations,
    expert_ids,
    route_weights,
    gain_dense,
    gain_expert,
    dense_gate,
    dense_up,
    dense_down,
    expert_gate,
    expert_up,
    expert_down,
):
    ny, nz = split
    chips = ny * nz
    half = ny // 2
    tokens, quarter = activations.shape[1:]
    full = quarter * tensors
    rows, dense_hidden = dense_gate.shape
    width = dense_hidden // ny
    slots = 2 * CAP
    hidden = expert_gate.shape[2]
    group = ny * tensors - 1
    steps = nz // 2
    bf16, f32 = jnp.bfloat16, jnp.float32
    dma = pltpu.SemaphoreType.DMA
    vmem = pl.BlockSpec(memory_space=pltpu.VMEM)
    hbm = pl.BlockSpec(memory_space=pl.ANY)
    sent_rows = (chips, slots, quarter)
    sections = pl.pallas_call(
        functools.partial(kernel, split, tensors),
        out_shape=jax.ShapeDtypeStruct((2, tokens, quarter), bf16),
        in_specs=[hbm] + [vmem] * 4 + [hbm] * 6,
        out_specs=vmem,
        scratch_shapes=[
            pltpu.VMEM((tokens, quarter), bf16),
            pltpu.VMEM((3, rows, dense_hidden), bf16),
            pltpu.VMEM((tensors, ny, tokens, quarter), bf16),
            pltpu.VMEM((chips, 3, rows, width), bf16),
            pltpu.VMEM((ny * tokens, width), bf16),
            pltpu.VMEM((tensors, ny, tokens, quarter), bf16),
            pltpu.VMEM((tensors - 1, ny, tokens // 2, quarter), bf16),
            pltpu.VMEM((ny - 1, tensors, tokens // 2, quarter), bf16),
            pltpu.VMEM((ny, tokens // 2, quarter), bf16),
            pltpu.VMEM((tensors, tokens // 2, quarter), bf16),
            pltpu.VMEM((ny - 1, tokens // 2, quarter), bf16),
            pltpu.VMEM((tensors - 1, tokens // 2, quarter), bf16),
            pltpu.VMEM((full, hidden), bf16),
            pltpu.VMEM((full, hidden), bf16),
            pltpu.VMEM((hidden, full), bf16),
            pltpu.VMEM((2, chips * slots, tokens), bf16),
            pltpu.VMEM((2, 2, tokens, chips * slots), bf16),
            pltpu.VMEM((2, tokens, quarter), bf16),
            pltpu.VMEM((tensors, 2, tokens, 128), f32),
            pltpu.VMEM(sent_rows, bf16),
            pltpu.VMEM((tensors, *sent_rows), bf16),
            pltpu.VMEM((tensors, *sent_rows), bf16),
            pltpu.VMEM((2, chips // 2, slots, quarter), bf16),
            pltpu.VMEM((2, *sent_rows), bf16),
            pltpu.VMEM(sent_rows, bf16),
            pltpu.VMEM(sent_rows, bf16),
            pltpu.VMEM((2, 2, tokens, quarter), f32),
            dma((7,)),
            dma((group,)),
            dma((group,)),
            dma((ny - 1, 3)),
            dma((half, 3)),
            dma((2, 2, half, steps)),
            dma((2, 2, half, steps)),
            dma((2, half, nz)),
            dma((2, half, nz)),
            dma((tensors - 1,)),
            dma((tensors - 1,)),
            dma((ny - 1, tensors)),
            dma((ny - 1, tensors)),
            dma((ny - 1,)),
            dma((ny - 1,)),
            dma((tensors - 1,)),
            dma((tensors - 1,)),
            dma(()),
            dma(()),
            dma((2 * tensors - 1,)),
            dma((2 * tensors - 1,)),
            dma((chips,)),
            dma((chips,)),
            dma((2, CHUNKS)),
            dma((2, CHUNKS)),
            dma((2, CHUNKS)),
            dma((2, CHUNKS)),
            dma((2, CHUNKS)),
            dma((2, CHUNKS)),
            dma((2, CHUNKS)),
            dma((2, CHUNKS)),
            dma((chips,)),
            dma((chips,)),
            dma(()),
            dma(()),
        ],
        compiler_params=pltpu.CompilerParams(
            collective_id=0, has_side_effects=True, vmem_limit_bytes=58 * 2**20
        ),
        name="sections",
    )(
        activations[0],
        expert_ids.transpose(2, 0, 1),
        route_weights.transpose(2, 0, 1),
        gain_dense,
        gain_expert,
        dense_gate,
        dense_up,
        dense_down,
        expert_gate,
        expert_up,
        expert_down,
    )
    return sections[None]


def solution(mesh, split=SPLIT):
    placed = (
        P("segment", "expert", "tensor"),
        P(None, "expert", None),
        P(None, "expert", None),
        P(),
        P(),
        P("expert", "tensor"),
        P("expert", "tensor"),
        P("expert", "tensor"),
        P("expert", None, "tensor"),
        P("expert", None, "tensor"),
        P("expert", "tensor", None),
    )
    return jax.shard_map(
        functools.partial(body, split, mesh.shape["tensor"]),
        mesh=mesh,
        in_specs=placed,
        out_specs=P("segment", None, "expert", "tensor"),
        check_vma=False,
    )
```

```python
import functools

import jax
import jax.numpy as jnp
from jax import lax
from jax.experimental import pallas as pl
from jax.experimental.pallas import tpu as pltpu
from jax.sharding import PartitionSpec as P

EPSILON = 1e-06
MESH = pl.DeviceIdType.MESH
CAP = 12
SPLIT = (4, 8)


def wait_bytes(ref, sem):
    pltpu.make_async_copy(ref, ref, sem).wait()


def places(split, tensors):
    ny, nz = split
    c, p, t = lax.axis_index("segment"), lax.axis_index("expert"), lax.axis_index("tensor")
    y, z = p // nz, p % nz

    def device(dc=0, dy=0, dz=0, dt=0):
        return (
            lax.rem(c + dc, 2),
            lax.rem(y + dy + ny, ny) * nz + lax.rem(z + dz + nz, nz),
            lax.rem(t + dt, tensors),
        )

    return c, p, t, y, z, device


def greet(offsets, device):
    barrier = pltpu.get_barrier_semaphore()
    for offset in offsets:
        pl.semaphore_signal(barrier, inc=1, device_id=device(*offset), device_id_type=MESH)
    pl.semaphore_wait(barrier, len(offsets))


def silu(v):
    return v / (1.0 + jnp.exp(-v))


def kernel(
    split,
    tensors,
    x_hbm,
    ids_ref,
    route_ref,
    gain_dense_ref,
    gain_expert_ref,
    dense_gate_hbm,
    dense_up_hbm,
    dense_down_hbm,
    gate_hbm,
    up_hbm,
    down_hbm,
    out_ref,
    x_ref,
    dense_held,
    xbuf,
    wbuf,
    hidden_ref,
    part,
    along_x,
    along_y,
    over_x,
    over_y,
    last_y,
    last_x,
    gate,
    up,
    down,
    place,
    mixers,
    mids,
    outgoing,
    arrived,
    pieces,
    through,
    beside,
    summed,
    returned,
    mixes,
    load_sem,
    tok_s,
    tok_r,
    w1_s,
    w1_r,
    ring_s,
    ring_r,
    sib_s,
    sib_r,
    a1_s,
    a1_r,
    b1_s,
    b1_r,
    a2_s,
    a2_r,
    b2_s,
    b2_r,
    mid_s,
    mid_r,
    go_s,
    go_r,
    x_s,
    x_r,
    f_s,
    f_r,
    half_s,
    half_r,
    side_s,
    side_r,
    back_s,
    back_r,
    mix_s,
    mix_r,
):
    ny, nz = split
    chips = ny * nz
    half = ny // 2
    c, p, t, y, z, device = places(split, tensors)
    tokens, quarter = x_ref.shape
    full = quarter * tensors
    rows, width = wbuf.shape[2:]
    per_quarter = quarter // rows
    slots = 2 * CAP
    all_slots = chips * slots
    hidden_width = gate.shape[1]
    right, left = 0, 1
    signs = (1, -1)
    first, second = pl.ds(0, tokens // 2), pl.ds(tokens // 2, tokens // 2)

    dense_loads = [
        pltpu.make_async_copy(far, dense_held.at[m], load_sem.at[m])
        for m, far in enumerate((dense_gate_hbm, dense_up_hbm, dense_down_hbm))
    ]
    dense_loads.append(pltpu.make_async_copy(x_hbm, x_ref, load_sem.at[3]))
    expert_loads = [
        pltpu.make_async_copy(far.at[c], near, load_sem.at[4 + i])
        for i, (far, near) in enumerate(((gate_hbm, gate), (up_hbm, up), (down_hbm, down)))
    ]
    for load in dense_loads + expert_loads:
        load.start()

    group = [(dy, dt) for dt in range(tensors) for dy in range(ny) if dy or dt]
    others = [(dc, dt) for dc in range(2) for dt in range(tensors) if dc or dt]
    offsets = {(0, dy, 0, dt) for dy, dt in group}
    offsets |= {(dc, 0, 0, dt) for dc, dt in others}
    offsets |= {(0, dy, dz, 0) for dy in range(ny) for dz in range(nz) if dy or dz}
    greet(sorted(offsets), device)
    for load in dense_loads:
        load.wait()

    started = []

    def send(src, dst, send_sem, recv_sem, to, keep=True):
        copy = pltpu.make_async_remote_copy(
            src_ref=src,
            dst_ref=dst,
            send_sem=send_sem,
            recv_sem=recv_sem,
            device_id=to,
            device_id_type=MESH,
        )
        copy.start()
        if keep:
            started.append(copy)

    def first_hop(m):
        copies = []
        for dy in range(1, ny):
            there = lax.rem(y + dy, ny)
            columns = pl.ds(pl.multiple_of(there * width, 128), width)
            copies.append(
                pltpu.make_async_remote_copy(
                    src_ref=dense_held.at[m, :, columns],
                    dst_ref=wbuf.at[p, m],
                    send_sem=w1_s.at[dy - 1, m],
                    recv_sem=w1_r.at[lax.rem(y, half), m],
                    device_id=device(0, dy, 0, 0),
                    device_id_type=MESH,
                )
            )
        return copies

    sends_weights = y // half == c

    @pl.when(sends_weights)
    def _():
        for m in range(3):
            for copy in first_hop(m):
                copy.start()
            columns = pl.ds(pl.multiple_of(y * width, 128), width)
            pltpu.make_async_copy(
                dense_held.at[m, :, columns], wbuf.at[p, m], w1_r.at[lax.rem(y, half), m]
            ).start()

    kinds = (pl.ds(0, 2), pl.ds(2, 1))
    hops = {}
    for a in range(half):
        far, near = nz // 2, (nz - 1) // 2
        hops[right, a], hops[left, a] = (far, near) if a % 2 == 0 else (near, far)

    def piece(core, a, dz):
        return (half * core + a) * nz + lax.rem(z + dz + nz, nz)

    def forward(kind, a, direction, step):
        sign = signs[direction]
        held = wbuf.at[piece(c, a, -sign * (step - 1)), kinds[kind]]
        send(
            held,
            held,
            ring_s.at[kind, direction, a, step - 1],
            ring_r.at[kind, direction, a, step - 1],
            device(0, 0, sign % nz, 0),
        )

    def hand_over(kind, a, dz):
        held = wbuf.at[piece(c, a, dz), kinds[kind]]
        send(held, held, sib_s.at[kind, a, dz % nz], sib_r.at[kind, a, dz % nz], device(1, 0, 0, 0))

    def begin(kind, a):
        for m in range(2) if kind == 0 else (2,):
            wait_bytes(wbuf.at[piece(c, a, 0), m], w1_r.at[a, m])
        for direction in (right, left):
            if hops[direction, a] >= 1:
                forward(kind, a, direction, 1)
        hand_over(kind, a, 0)

    def ring(kind, a, step):
        for direction in (right, left):
            if step > hops[direction, a]:
                continue
            sign = signs[direction]
            wait_bytes(
                wbuf.at[piece(c, a, -sign * step), kinds[kind]],
                ring_r.at[kind, direction, a, step - 1],
            )
            if step + 1 <= hops[direction, a]:
                forward(kind, a, direction, step + 1)
            hand_over(kind, a, -sign * step)

    def from_other_core(kind, a):
        for dz in range(nz):
            wait_bytes(wbuf.at[piece(1 - c, a, dz), kinds[kind]], sib_r.at[kind, a, dz])

    for a in range(half):
        begin(0, a)

    for i, (dy, dt) in enumerate(group):
        send(x_ref, xbuf.at[t, y], tok_s.at[i], tok_r.at[i], device(0, dy, 0, dt))
    xbuf[t, y] = x_ref[...]

    per = nz // 2
    chunks = 2 * ny
    self_k = chips - per

    def offset(k):
        chunk = k // per
        dy = (chunk // 2 + 1) % ny
        i = (chunk + chunk // (chunks - 2)) % 2 * per + k % per
        dz = i % 2 * ((i + 1) // 2) + (i + 1) % 2 * ((nz - i // 2) % nz)
        return dy, dz

    def expert_at(k):
        dy, dz = offset(k)
        there = (y + dy) % ny * nz + (z + dz) % nz
        return 2 * there + c

    def iotas(shape):
        return (lax.broadcasted_iota(jnp.int32, shape, i) for i in range(2))

    def plan_routes():
        experts = expert_at(lax.broadcasted_iota(jnp.int32, (chips, tokens), 0))
        one, two = iotas((tokens, tokens))
        before = jnp.where(one < two, 1.0, 0.0).astype(jnp.bfloat16)
        slot, chip = iotas((all_slots, chips))
        spread_t = jnp.where(slot // slots == chip, 1.0, 0.0).astype(jnp.bfloat16)

        def chosen(found, slot, m):
            rank = jnp.where((slot // CAP) % 2 == m, slot % CAP, 2 * tokens)
            return found == rank.astype(jnp.float32)

        for m in range(2):
            named = jnp.zeros((chips, tokens), jnp.float32)
            share = jnp.zeros((chips, tokens), jnp.float32)
            for j in range(ids_ref.shape[0]):
                same = ids_ref[j, m : m + 1, :] == experts
                named += jnp.where(same, 1.0, 0.0)
                share += jnp.where(same, route_ref[j, m : m + 1, :], 0.0)
            ranks = jnp.dot(
                named.astype(jnp.bfloat16), before, preferred_element_type=jnp.float32
            )
            ranks = jnp.where(named > 0.5, ranks, -1.0)
            found = jnp.dot(
                spread_t, ranks.astype(jnp.bfloat16), preferred_element_type=jnp.float32
            )
            slot, token = iotas((all_slots, tokens))
            place[m] = jnp.where(chosen(found, slot, m), 1.0, 0.0).astype(jnp.bfloat16)
            ranks_t, share_t = ranks.T.astype(jnp.bfloat16), share.T
            high = share_t.astype(jnp.bfloat16)
            low = (share_t - high.astype(jnp.float32)).astype(jnp.bfloat16)
            for g in range(4):
                chip, slot = iotas((chips, all_slots // 4))
                spread = jnp.where(slot // slots + g * (chips // 4) == chip, 1.0, 0.0)
                spread = spread.astype(jnp.bfloat16)
                found = jnp.dot(ranks_t, spread, preferred_element_type=jnp.float32)
                token, slot = iotas((tokens, all_slots // 4))
                here = chosen(found, slot, m)
                for i, values in enumerate((high, low)):
                    values = jnp.dot(values, spread, preferred_element_type=jnp.float32)
                    mixers[g, m, i] = jnp.where(here, values, 0.0).astype(jnp.bfloat16)

    def norm_block(j, carry):
        squares = jnp.zeros((tokens, 1), jnp.float32)
        for q in range(tensors):
            values = xbuf[q, j].astype(jnp.float32)
            squares += jnp.sum(values * values, axis=1, keepdims=True)
        inverse = lax.rsqrt(squares / full + EPSILON)
        for q in range(tensors):
            values = xbuf[q, j].astype(jnp.float32)
            gain = gain_dense_ref[q * quarter : (q + 1) * quarter].reshape(1, quarter)
            xbuf[q, j] = (values * inverse * gain).astype(jnp.bfloat16)
        return carry

    acc = [jnp.zeros((ny * tokens, width), jnp.float32) for _ in range(2)]

    def add_quarter(q):
        normed = xbuf[q].reshape(ny * tokens, quarter)
        held = pl.ds(q * per_quarter, per_quarter)
        for i in range(2):
            acc[i] += jnp.dot(
                normed, wbuf[held, i].reshape(quarter, width), preferred_element_type=jnp.float32
            )

    def give_quarter(q):
        held = wbuf[pl.ds(q * per_quarter, per_quarter), 2].reshape(quarter, width)
        result = lax.dot_general(
            hidden_ref[...], held, (((1,), (1,)), ((), ())), preferred_element_type=jnp.float32
        )
        part[q] = result.astype(jnp.bfloat16).reshape(ny, tokens, quarter)
        for dy in range(1, ny):
            send(
                part.at[q, lax.rem(y + dy, ny), second],
                along_y.at[dy - 1, q],
                b1_s.at[dy - 1, q],
                b1_r.at[dy - 1, q],
                device(0, dy, 0, 0),
                keep=False,
            )
        dt = lax.rem(q - t + tensors, tensors)

        @pl.when(dt > 0)
        def _():
            send(
                part.at[q, :, first],
                along_x.at[dt - 1],
                a1_s.at[dt - 1],
                a1_r.at[dt - 1],
                device(0, 0, 0, dt),
                keep=False,
            )

    def quarters(a):
        last = [((q + 1) * per_quarter - 1) // nz % half for q in range(tensors)]
        return [q for q in range(tensors) if last[q] == a]

    steps = nz // 2
    early = max(steps - 1, 1)
    for step in range(1, steps + 1):
        for a in range(half):
            ring(0, a, step)
        if step == early:
            begin(1, 0)
            for i in range(len(group)):
                wait_bytes(xbuf.at[0, 0], tok_r.at[i])
            lax.fori_loop(0, ny, norm_block, 0)
        if step == steps and half > 1:
            begin(1, half - 1)
    left_over = list(range(tensors))
    for step in range(1, steps + 1):
        ring(1, 0, step)
        if half > 1 and step < steps:
            ring(1, half - 1, step)
        if step == 1:
            for a in range(half):
                from_other_core(0, a)
        if step < steps and left_over:
            add_quarter(left_over.pop(0))
    for q in left_over:
        add_quarter(q)
    hidden_ref[...] = (silu(acc[0]) * acc[1]).astype(jnp.bfloat16)
    for a in range(half):
        if a:
            ring(1, a, steps)
        from_other_core(1, a)
        for q in quarters(a):
            give_quarter(q)
    plan_routes()

    total = part[t, :, first].astype(jnp.float32)
    for i in range(tensors - 1):
        wait_bytes(along_x.at[i], a1_r.at[i])
        total += along_x[i].astype(jnp.float32)
    over_x[...] = total.astype(jnp.bfloat16)
    for dy in range(1, ny):
        send(
            over_x.at[lax.rem(y + dy, ny)],
            last_y.at[dy - 1],
            a2_s.at[dy - 1],
            a2_r.at[dy - 1],
            device(0, dy, 0, 0),
        )
    total = part[:, y, second].astype(jnp.float32)
    for dy in range(1, ny):
        for q in range(tensors):
            wait_bytes(along_y.at[dy - 1, q], b1_r.at[dy - 1, q])
        total += along_y[dy - 1].astype(jnp.float32)
    over_y[...] = total.astype(jnp.bfloat16)
    for dt in range(1, tensors):
        send(
            over_y.at[lax.rem(t + dt, tensors)],
            last_x.at[dt - 1],
            b2_s.at[dt - 1],
            b2_r.at[dt - 1],
            device(0, 0, 0, dt),
        )
    upper = over_x[y].astype(jnp.float32)
    for dy in range(1, ny):
        wait_bytes(last_y.at[dy - 1], a2_r.at[dy - 1])
        upper += last_y[dy - 1].astype(jnp.float32)
    lower = over_y[t].astype(jnp.float32)
    for dt in range(1, tensors):
        wait_bytes(last_x.at[dt - 1], b2_r.at[dt - 1])
        lower += last_x[dt - 1].astype(jnp.float32)
    total = jnp.concatenate([upper, lower], axis=0)
    own = (x_ref[...].astype(jnp.float32) + total).astype(jnp.bfloat16)

    mids[c] = own
    send(mids.at[c], mids.at[c], mid_s, mid_r, device(1, 0, 0, 0))
    wait_bytes(mids.at[0], mid_r)

    for chunk in range(chunks):
        these = pl.ds(chunk * per * slots, per * slots)
        block = jnp.dot(place[0, these], mids[0], preferred_element_type=jnp.float32)
        block += jnp.dot(place[1, these], mids[1], preferred_element_type=jnp.float32)
        block = block.reshape(per, slots, quarter).astype(jnp.bfloat16)
        outgoing[pl.ds(chunk * per, per)] = block
        low = chunk * per
        if low == self_k:
            arrived[t, self_k] = block[0]

        def go(k, carry):
            send(
                outgoing.at[k],
                arrived.at[t, k],
                go_s.at[k],
                go_r.at[k],
                device(0, *offset(k), 0),
                keep=False,
            )
            return carry

        lax.fori_loop(low + (low == self_k), low + per, go, 0)

    for load in expert_loads:
        load.wait()
    for copy in started:
        copy.wait_send()
    for i in range(tensors - 1):
        wait_bytes(along_x.at[i], a1_s.at[i])
    for dy in range(ny - 1):
        for q in range(tensors):
            wait_bytes(along_y.at[dy, q], b1_s.at[dy, q])

    @pl.when(sends_weights)
    def _():
        for m in range(3):
            for copy in first_hop(m):
                copy.wait_send()

    cut = per // 2
    ways = ((right, 1), (left, tensors - 1))
    far_away = tensors // 2

    def some(chunk):
        return pl.ds(chunk * per, per)

    def half_of(chunk, way):
        return pl.ds(chunk * per + way * cut, cut)

    def back_to(k):
        dy, dz = offset(k)
        return device(0, ny - dy, nz - dz, 0)

    def share_chunk(chunk):
        def arrive(i, carry):
            k = chunk * per + i

            @pl.when(k != self_k)
            def _():
                wait_bytes(arrived.at[t, k], go_r.at[k])

            return carry

        lax.fori_loop(0, per, arrive, 0)
        held = arrived.at[t, some(chunk)]
        for way, dt in ways:
            send(held, held, x_s.at[way, chunk], x_r.at[way, chunk], device(0, 0, 0, dt), False)

    def forward_chunk(chunk):
        for way, dt in ways:
            source = lax.rem(t + tensors - dt, tensors)
            wait_bytes(arrived.at[source, some(chunk)], x_r.at[way, chunk])
            held = arrived.at[source, half_of(chunk, way)]
            send(held, held, f_s.at[way, chunk], f_r.at[way, chunk], device(0, 0, 0, dt), False)

    def compute_chunk(chunk):
        here = some(chunk)
        source = lax.rem(t + far_away, tensors)
        for way, dt in ways:
            wait_bytes(arrived.at[source, half_of(chunk, way)], f_r.at[way, chunk])
        gate_sums = jnp.zeros((per * slots, hidden_width), jnp.float32)
        upward = jnp.zeros((per * slots, hidden_width), jnp.float32)
        squares = jnp.zeros((per, slots, 1), jnp.float32)
        for q in range(tensors):
            values = arrived[q, here].astype(jnp.float32)
            squares += jnp.sum(values * values, axis=2, keepdims=True)
        inverse = lax.rsqrt(squares / full + EPSILON)
        for q in range(tensors):
            these = slice(q * quarter, (q + 1) * quarter)
            gain = gain_expert_ref[these].reshape(1, 1, quarter)
            values = arrived[q, here].astype(jnp.float32) * inverse * gain
            values = values.reshape(per * slots, quarter).astype(jnp.bfloat16)
            gate_sums += jnp.dot(values, gate[these], preferred_element_type=jnp.float32)
            upward += jnp.dot(values, up[these], preferred_element_type=jnp.float32)
        hidden = (silu(gate_sums) * upward).astype(jnp.bfloat16)
        for dt in (far_away, 1, tensors - 1, 0):
            there = lax.rem(t + dt, tensors)
            columns = pl.ds(pl.multiple_of(there * quarter, 128), quarter)
            result = jnp.dot(hidden, down[:, columns], preferred_element_type=jnp.float32)
            pieces[dt, here] = result.reshape(per, slots, quarter).astype(jnp.bfloat16)
            if dt == far_away:
                for way, near in ways:
                    send(
                        pieces.at[dt, half_of(chunk, way)],
                        through.at[way, pl.ds(chunk * cut, cut)],
                        half_s.at[way, chunk],
                        half_r.at[way, chunk],
                        device(0, 0, 0, near),
                        False,
                    )

    def relay_chunk(chunk):
        for way, dt in ways:
            came = pl.ds(chunk * cut, cut)
            wait_bytes(through.at[way, came], half_r.at[way, chunk])
            these = half_of(chunk, way)
            both = pieces[dt, these].astype(jnp.float32) + through[way, came].astype(jnp.float32)
            pieces[dt, these] = both.astype(jnp.bfloat16)
            send(
                pieces.at[dt, some(chunk)],
                beside.at[way, some(chunk)],
                side_s.at[way, chunk],
                side_r.at[way, chunk],
                device(0, 0, 0, dt),
                False,
            )

    def return_chunk(chunk):
        here = some(chunk)
        total = pieces[0, here].astype(jnp.float32)
        for way, dt in ways:
            wait_bytes(beside.at[way, here], side_r.at[way, chunk])
            total += beside[way, here].astype(jnp.float32)
        summed[here] = total.astype(jnp.bfloat16)

        def give(i, carry):
            k = chunk * per + i

            @pl.when(k != self_k)
            def _():
                send(
                    summed.at[k],
                    returned.at[k],
                    back_s.at[k],
                    back_r.at[k],
                    back_to(k),
                    False,
                )

            return carry

        lax.fori_loop(0, per, give, 0)

    work = ((0, share_chunk), (1, forward_chunk), (2, compute_chunk), (3, relay_chunk), (4, return_chunk))

    def stage(i, carry):
        for lag, act in work:

            @pl.when((i >= lag) & (i < chunks + lag))
            def _(lag=lag, act=act):
                act(i - lag)

        return carry

    lax.fori_loop(0, chunks + len(work) - 1, stage, 0)
    returned[self_k] = summed[self_k]

    def sent_rows(k, carry):
        wait_bytes(outgoing.at[k], go_s.at[k])
        return carry

    lax.fori_loop(0, self_k, sent_rows, 0)
    lax.fori_loop(self_k + 1, chips, sent_rows, 0)

    def sent_chunk(chunk, carry):
        for way, dt in ways:
            wait_bytes(arrived.at[0, some(chunk)], x_s.at[way, chunk])
            wait_bytes(arrived.at[0, half_of(chunk, way)], f_s.at[way, chunk])
            wait_bytes(arrived.at[0, half_of(chunk, way)], half_s.at[way, chunk])
            wait_bytes(pieces.at[0, some(chunk)], side_s.at[way, chunk])
        return carry

    lax.fori_loop(0, chunks, sent_chunk, 0)

    def arrive_back(k, carry):
        wait_bytes(returned.at[k], back_r.at[k])
        return carry

    mixed = [jnp.zeros((tokens, quarter), jnp.float32) for _ in range(2)]
    for g in range(4):
        low, high = g * chips // 4, (g + 1) * chips // 4
        lax.fori_loop(low, min(high, self_k), arrive_back, 0)
        lax.fori_loop(max(low, self_k + 1), high, arrive_back, 0)
        back = returned[low:high].reshape(all_slots // 4, quarter)
        for m in range(2):
            for j in range(2):
                mixed[m] += jnp.dot(mixers[g, m, j], back, preferred_element_type=jnp.float32)
    for m in range(2):
        mixes[0, m] = mixed[m]
    send(mixes.at[0], mixes.at[1], mix_s, mix_r, device(1, 0, 0, 0), False)
    wait_bytes(mixes.at[1], mix_r)
    for m in range(2):
        middle = mids[m]
        final = middle.astype(jnp.float32) + (mixes[0, m] + mixes[1, m])
        out_ref[m] = jnp.where(c == 0, middle, final.astype(jnp.bfloat16))

    wait_bytes(mixes.at[0], mix_s)

    def sent(k, carry):
        wait_bytes(summed.at[k], back_s.at[k])
        return carry

    lax.fori_loop(0, self_k, sent, 0)
    lax.fori_loop(self_k + 1, chips, sent, 0)


def body(
    split,
    tensors,
    activations,
    expert_ids,
    route_weights,
    gain_dense,
    gain_expert,
    dense_gate,
    dense_up,
    dense_down,
    expert_gate,
    expert_up,
    expert_down,
):
    ny, nz = split
    chips = ny * nz
    half = ny // 2
    tokens, quarter = activations.shape[1:]
    full = quarter * tensors
    rows, dense_hidden = dense_gate.shape
    width = dense_hidden // ny
    slots = 2 * CAP
    hidden = expert_gate.shape[2]
    group = ny * tensors - 1
    steps = nz // 2
    bf16, f32 = jnp.bfloat16, jnp.float32
    dma = pltpu.SemaphoreType.DMA
    vmem = pl.BlockSpec(memory_space=pltpu.VMEM)
    hbm = pl.BlockSpec(memory_space=pl.ANY)
    sent_rows = (chips, slots, quarter)
    sections = pl.pallas_call(
        functools.partial(kernel, split, tensors),
        out_shape=jax.ShapeDtypeStruct((2, tokens, quarter), bf16),
        in_specs=[hbm] + [vmem] * 4 + [hbm] * 6,
        out_specs=vmem,
        scratch_shapes=[
            pltpu.VMEM((tokens, quarter), bf16),
            pltpu.VMEM((3, rows, dense_hidden), bf16),
            pltpu.VMEM((tensors, ny, tokens, quarter), bf16),
            pltpu.VMEM((chips, 3, rows, width), bf16),
            pltpu.VMEM((ny * tokens, width), bf16),
            pltpu.VMEM((tensors, ny, tokens, quarter), bf16),
            pltpu.VMEM((tensors - 1, ny, tokens // 2, quarter), bf16),
            pltpu.VMEM((ny - 1, tensors, tokens // 2, quarter), bf16),
            pltpu.VMEM((ny, tokens // 2, quarter), bf16),
            pltpu.VMEM((tensors, tokens // 2, quarter), bf16),
            pltpu.VMEM((ny - 1, tokens // 2, quarter), bf16),
            pltpu.VMEM((tensors - 1, tokens // 2, quarter), bf16),
            pltpu.VMEM((full, hidden), bf16),
            pltpu.VMEM((full, hidden), bf16),
            pltpu.VMEM((hidden, full), bf16),
            pltpu.VMEM((2, chips * slots, tokens), bf16),
            pltpu.VMEM((4, 2, 2, tokens, chips // 4 * slots), bf16),
            pltpu.VMEM((2, tokens, quarter), bf16),
            pltpu.VMEM(sent_rows, bf16),
            pltpu.VMEM((tensors, *sent_rows), bf16),
            pltpu.VMEM((tensors, *sent_rows), bf16),
            pltpu.VMEM((2, chips // 2, slots, quarter), bf16),
            pltpu.VMEM((2, *sent_rows), bf16),
            pltpu.VMEM(sent_rows, bf16),
            pltpu.VMEM(sent_rows, bf16),
            pltpu.VMEM((2, 2, tokens, quarter), f32),
            dma((7,)),
            dma((group,)),
            dma((group,)),
            dma((ny - 1, 3)),
            dma((half, 3)),
            dma((2, 2, half, steps)),
            dma((2, 2, half, steps)),
            dma((2, half, nz)),
            dma((2, half, nz)),
            dma((tensors - 1,)),
            dma((tensors - 1,)),
            dma((ny - 1, tensors)),
            dma((ny - 1, tensors)),
            dma((ny - 1,)),
            dma((ny - 1,)),
            dma((tensors - 1,)),
            dma((tensors - 1,)),
            dma(()),
            dma(()),
            dma((chips,)),
            dma((chips,)),
            dma((2, 2 * ny)),
            dma((2, 2 * ny)),
            dma((2, 2 * ny)),
            dma((2, 2 * ny)),
            dma((2, 2 * ny)),
            dma((2, 2 * ny)),
            dma((2, 2 * ny)),
            dma((2, 2 * ny)),
            dma((chips,)),
            dma((chips,)),
            dma(()),
            dma(()),
        ],
        compiler_params=pltpu.CompilerParams(
            collective_id=0, has_side_effects=True, vmem_limit_bytes=58 * 2**20
        ),
        name="sections",
    )(
        activations[0],
        expert_ids.transpose(2, 0, 1),
        route_weights.transpose(2, 0, 1),
        gain_dense,
        gain_expert,
        dense_gate,
        dense_up,
        dense_down,
        expert_gate,
        expert_up,
        expert_down,
    )
    return sections[None]


def solution(mesh, split=SPLIT):
    placed = (
        P("segment", "expert", "tensor"),
        P(None, "expert", None),
        P(None, "expert", None),
        P(),
        P(),
        P("expert", "tensor"),
        P("expert", "tensor"),
        P("expert", "tensor"),
        P("expert", None, "tensor"),
        P("expert", None, "tensor"),
        P("expert", "tensor", None),
    )
    return jax.shard_map(
        functools.partial(body, split, mesh.shape["tensor"]),
        mesh=mesh,
        in_specs=placed,
        out_specs=P("segment", None, "expert", "tensor"),
        check_vma=False,
    )
```

```python
import functools

import jax
import jax.numpy as jnp
from jax import lax
from jax.experimental import pallas as pl
from jax.experimental.pallas import tpu as pltpu
from jax.sharding import PartitionSpec as P

EPSILON = 1e-06
MESH = pl.DeviceIdType.MESH
CAP = 12
SPLIT = (4, 8)


def wait_bytes(ref, sem):
    pltpu.make_async_copy(ref, ref, sem).wait()


def places(split, tensors):
    ny, nz = split
    c, p, t = lax.axis_index("segment"), lax.axis_index("expert"), lax.axis_index("tensor")
    y, z = p // nz, p % nz

    def device(dc=0, dy=0, dz=0, dt=0):
        return (
            lax.rem(c + dc, 2),
            lax.rem(y + dy + ny, ny) * nz + lax.rem(z + dz + nz, nz),
            lax.rem(t + dt, tensors),
        )

    return c, p, t, y, z, device


def greet(offsets, device):
    barrier = pltpu.get_barrier_semaphore()
    for offset in offsets:
        pl.semaphore_signal(barrier, inc=1, device_id=device(*offset), device_id_type=MESH)
    pl.semaphore_wait(barrier, len(offsets))


def silu(v):
    return v / (1.0 + jnp.exp(-v))


def kernel(
    split,
    tensors,
    x_hbm,
    ids_ref,
    route_ref,
    gain_dense_ref,
    gain_expert_ref,
    dense_gate_hbm,
    dense_up_hbm,
    dense_down_hbm,
    gate_hbm,
    up_hbm,
    down_hbm,
    out_ref,
    x_ref,
    dense_held,
    xbuf,
    wbuf,
    hidden_ref,
    part,
    along_x,
    along_y,
    over_x,
    over_y,
    last_y,
    last_x,
    gate,
    up,
    down,
    place,
    mixers,
    mids,
    outgoing,
    arrived,
    pieces,
    through,
    beside,
    summed,
    returned,
    mixes,
    load_sem,
    tok_s,
    tok_r,
    w1_s,
    w1_r,
    ring_s,
    ring_r,
    sib_s,
    sib_r,
    a1_s,
    a1_r,
    b1_s,
    b1_r,
    a2_s,
    a2_r,
    b2_s,
    b2_r,
    mid_s,
    mid_r,
    go_s,
    go_r,
    x_s,
    x_r,
    f_s,
    f_r,
    half_s,
    half_r,
    side_s,
    side_r,
    back_s,
    back_r,
    mix_s,
    mix_r,
):
    ny, nz = split
    chips = ny * nz
    half = ny // 2
    c, p, t, y, z, device = places(split, tensors)
    tokens, quarter = x_ref.shape
    full = quarter * tensors
    rows, width = wbuf.shape[2:]
    per_quarter = quarter // rows
    slots = 2 * CAP
    all_slots = chips * slots
    hidden_width = gate.shape[1]
    right, left = 0, 1
    signs = (1, -1)
    first, second = pl.ds(0, tokens // 2), pl.ds(tokens // 2, tokens // 2)

    dense_loads = [
        pltpu.make_async_copy(far, dense_held.at[m], load_sem.at[m])
        for m, far in enumerate((dense_gate_hbm, dense_up_hbm, dense_down_hbm))
    ]
    dense_loads.append(pltpu.make_async_copy(x_hbm, x_ref, load_sem.at[3]))
    expert_loads = [
        pltpu.make_async_copy(far.at[c], near, load_sem.at[4 + i])
        for i, (far, near) in enumerate(((gate_hbm, gate), (up_hbm, up), (down_hbm, down)))
    ]
    for load in dense_loads + expert_loads:
        load.start()

    group = [(dy, dt) for dt in range(tensors) for dy in range(ny) if dy or dt]
    offsets = {(0, dy, 0, dt) for dy, dt in group}
    offsets |= {(1, 0, 0, 0)}
    offsets |= {(0, dy, dz, 0) for dy in range(ny) for dz in range(nz) if dy or dz}
    greet(sorted(offsets), device)
    for load in dense_loads:
        load.wait()

    started = []

    def send(src, dst, send_sem, recv_sem, to, keep=True):
        copy = pltpu.make_async_remote_copy(
            src_ref=src,
            dst_ref=dst,
            send_sem=send_sem,
            recv_sem=recv_sem,
            device_id=to,
            device_id_type=MESH,
        )
        copy.start()
        if keep:
            started.append(copy)

    def first_hop(m):
        copies = []
        for dy in range(1, ny):
            there = lax.rem(y + dy, ny)
            columns = pl.ds(pl.multiple_of(there * width, 128), width)
            copies.append(
                pltpu.make_async_remote_copy(
                    src_ref=dense_held.at[m, :, columns],
                    dst_ref=wbuf.at[p, m],
                    send_sem=w1_s.at[dy - 1, m],
                    recv_sem=w1_r.at[lax.rem(y, half), m],
                    device_id=device(0, dy, 0, 0),
                    device_id_type=MESH,
                )
            )
        return copies

    sends_weights = y // half == c

    @pl.when(sends_weights)
    def _():
        for m in range(3):
            for copy in first_hop(m):
                copy.start()
            columns = pl.ds(pl.multiple_of(y * width, 128), width)
            pltpu.make_async_copy(
                dense_held.at[m, :, columns], wbuf.at[p, m], w1_r.at[lax.rem(y, half), m]
            ).start()

    hops = {}
    for a in range(half):
        far, near = nz // 2, (nz - 1) // 2
        hops[right, a], hops[left, a] = (far, near) if a % 2 == 0 else (near, far)

    def piece(core, a, dz):
        return (half * core + a) * nz + lax.rem(z + dz + nz, nz)

    def forward(kind, a, direction, step):
        sign = signs[direction]
        held = wbuf.at[piece(c, a, -sign * (step - 1)), kind]
        send(
            held,
            held,
            ring_s.at[kind, direction, a, step - 1],
            ring_r.at[kind, direction, a, step - 1],
            device(0, 0, sign % nz, 0),
        )

    def hand_over(kind, a, dz):
        held = wbuf.at[piece(c, a, dz), kind]
        send(held, held, sib_s.at[kind, a, dz % nz], sib_r.at[kind, a, dz % nz], device(1, 0, 0, 0))

    def begin(kind, a):
        wait_bytes(wbuf.at[piece(c, a, 0), kind], w1_r.at[a, kind])
        for direction in (right, left):
            if hops[direction, a] >= 1:
                forward(kind, a, direction, 1)
        hand_over(kind, a, 0)

    def ring(kind, a, step):
        for direction in (right, left):
            if step > hops[direction, a]:
                continue
            sign = signs[direction]
            wait_bytes(
                wbuf.at[piece(c, a, -sign * step), kind],
                ring_r.at[kind, direction, a, step - 1],
            )
            if step + 1 <= hops[direction, a]:
                forward(kind, a, direction, step + 1)
            hand_over(kind, a, -sign * step)

    def from_other_core(kind, a):
        for dz in range(nz):
            wait_bytes(wbuf.at[piece(1 - c, a, dz), kind], sib_r.at[kind, a, dz])

    for kind in range(2):
        for a in range(half):
            begin(kind, a)

    for i, (dy, dt) in enumerate(group):
        send(x_ref, xbuf.at[t, y], tok_s.at[i], tok_r.at[i], device(0, dy, 0, dt))
    xbuf[t, y] = x_ref[...]

    per = nz // 2
    chunks = 2 * ny
    self_k = chips - per

    def offset(k):
        chunk = k // per
        dy = (chunk // 2 + 1) % ny
        i = (chunk + chunk // (chunks - 2)) % 2 * per + k % per
        dz = i % 2 * ((i + 1) // 2) + (i + 1) % 2 * ((nz - i // 2) % nz)
        return dy, dz

    def expert_at(k):
        dy, dz = offset(k)
        there = (y + dy) % ny * nz + (z + dz) % nz
        return 2 * there + c

    def iotas(shape):
        return (lax.broadcasted_iota(jnp.int32, shape, i) for i in range(2))

    def mix_plan(m, ranks, share, chosen):
        ranks_t, share_t = ranks.T.astype(jnp.bfloat16), share.T
        high = share_t.astype(jnp.bfloat16)
        low = (share_t - high.astype(jnp.float32)).astype(jnp.bfloat16)
        for g in range(4):
            chip, slot = iotas((chips, all_slots // 4))
            spread = jnp.where(slot // slots + g * (chips // 4) == chip, 1.0, 0.0)
            spread = spread.astype(jnp.bfloat16)
            found = jnp.dot(ranks_t, spread, preferred_element_type=jnp.float32)
            token, slot = iotas((tokens, all_slots // 4))
            here = chosen(found, slot, m)
            for i, values in enumerate((high, low)):
                values = jnp.dot(values, spread, preferred_element_type=jnp.float32)
                mixers[g, m, i] = jnp.where(here, values, 0.0).astype(jnp.bfloat16)

    def plan_routes(mixing):
        experts = expert_at(lax.broadcasted_iota(jnp.int32, (chips, tokens), 0))
        one, two = iotas((tokens, tokens))
        before = jnp.where(one < two, 1.0, 0.0).astype(jnp.bfloat16)
        slot, chip = iotas((all_slots, chips))
        spread_t = jnp.where(slot // slots == chip, 1.0, 0.0).astype(jnp.bfloat16)

        def chosen(found, slot, m):
            rank = jnp.where((slot // CAP) % 2 == m, slot % CAP, 2 * tokens)
            return found == rank.astype(jnp.float32)

        for m in range(2):
            named = jnp.zeros((chips, tokens), jnp.float32)
            share = jnp.zeros((chips, tokens), jnp.float32)
            for j in range(ids_ref.shape[0]):
                same = ids_ref[j, m : m + 1, :] == experts
                named += jnp.where(same, 1.0, 0.0)
                share += jnp.where(same, route_ref[j, m : m + 1, :], 0.0)
            ranks = jnp.dot(
                named.astype(jnp.bfloat16), before, preferred_element_type=jnp.float32
            )
            ranks = jnp.where(named > 0.5, ranks, -1.0)
            if mixing:
                mix_plan(m, ranks, share, chosen)
                continue
            found = jnp.dot(
                spread_t, ranks.astype(jnp.bfloat16), preferred_element_type=jnp.float32
            )
            slot, token = iotas((all_slots, tokens))
            place[m] = jnp.where(chosen(found, slot, m), 1.0, 0.0).astype(jnp.bfloat16)

    def norm_block(j, carry):
        squares = jnp.zeros((tokens, 1), jnp.float32)
        for q in range(tensors):
            values = xbuf[q, j].astype(jnp.float32)
            squares += jnp.sum(values * values, axis=1, keepdims=True)
        inverse = lax.rsqrt(squares / full + EPSILON)
        for q in range(tensors):
            values = xbuf[q, j].astype(jnp.float32)
            gain = gain_dense_ref[q * quarter : (q + 1) * quarter].reshape(1, quarter)
            xbuf[q, j] = (values * inverse * gain).astype(jnp.bfloat16)
        return carry

    acc = [jnp.zeros((ny * tokens, width), jnp.float32) for _ in range(2)]

    def add_quarter(q):
        normed = xbuf[q].reshape(ny * tokens, quarter)
        held = pl.ds(q * per_quarter, per_quarter)
        for i in range(2):
            acc[i] += jnp.dot(
                normed, wbuf[held, i].reshape(quarter, width), preferred_element_type=jnp.float32
            )

    def give_quarter(q):
        held = wbuf[pl.ds(q * per_quarter, per_quarter), 2].reshape(quarter, width)
        result = lax.dot_general(
            hidden_ref[...], held, (((1,), (1,)), ((), ())), preferred_element_type=jnp.float32
        )
        part[q] = result.astype(jnp.bfloat16).reshape(ny, tokens, quarter)
        for dy in range(1, ny):
            send(
                part.at[q, lax.rem(y + dy, ny), second],
                along_y.at[dy - 1, q],
                b1_s.at[dy - 1, q],
                b1_r.at[dy - 1, q],
                device(0, dy, 0, 0),
                keep=False,
            )
        dt = lax.rem(q - t + tensors, tensors)

        @pl.when(dt > 0)
        def _():
            send(
                part.at[q, :, first],
                along_x.at[dt - 1],
                a1_s.at[dt - 1],
                a1_r.at[dt - 1],
                device(0, 0, 0, dt),
                keep=False,
            )

    def quarters(a):
        last = [((q + 1) * per_quarter - 1) // nz % half for q in range(tensors)]
        return [q for q in range(tensors) if last[q] == a]

    steps = nz // 2
    early = max(steps - 1, 1)
    for step in range(1, steps + 1):
        for kind in range(2):
            for a in range(half):
                ring(kind, a, step)
        if step == max(steps - 2, 1):
            begin(2, 0)
        if step == early and half > 1:
            begin(2, half - 1)
        if step == early:
            for i in range(len(group)):
                wait_bytes(xbuf.at[0, 0], tok_r.at[i])
            lax.fori_loop(0, ny, norm_block, 0)
    left_over = list(range(tensors))
    for step in range(1, steps + 1):
        ring(2, 0, step)
        if half > 1 and step < steps:
            ring(2, half - 1, step)
        if step == 1:
            for a in range(half):
                from_other_core(0, a)
                from_other_core(1, a)
        if step < steps and left_over:
            add_quarter(left_over.pop(0))
    for q in left_over:
        add_quarter(q)
    hidden_ref[...] = (silu(acc[0]) * acc[1]).astype(jnp.bfloat16)
    for a in range(half):
        if a:
            ring(2, a, steps)
        from_other_core(2, a)
        for q in quarters(a):
            give_quarter(q)
    plan_routes(False)

    total = part[t, :, first].astype(jnp.float32)
    for i in range(tensors - 1):
        wait_bytes(along_x.at[i], a1_r.at[i])
        total += along_x[i].astype(jnp.float32)
    over_x[...] = total.astype(jnp.bfloat16)
    for dy in range(1, ny):
        send(
            over_x.at[lax.rem(y + dy, ny)],
            last_y.at[dy - 1],
            a2_s.at[dy - 1],
            a2_r.at[dy - 1],
            device(0, dy, 0, 0),
        )
    total = part[:, y, second].astype(jnp.float32)
    for dy in range(1, ny):
        for q in range(tensors):
            wait_bytes(along_y.at[dy - 1, q], b1_r.at[dy - 1, q])
        total += along_y[dy - 1].astype(jnp.float32)
    over_y[...] = total.astype(jnp.bfloat16)
    for dt in range(1, tensors):
        send(
            over_y.at[lax.rem(t + dt, tensors)],
            last_x.at[dt - 1],
            b2_s.at[dt - 1],
            b2_r.at[dt - 1],
            device(0, 0, 0, dt),
        )
    upper = over_x[y].astype(jnp.float32)
    for dy in range(1, ny):
        wait_bytes(last_y.at[dy - 1], a2_r.at[dy - 1])
        upper += last_y[dy - 1].astype(jnp.float32)
    lower = over_y[t].astype(jnp.float32)
    for dt in range(1, tensors):
        wait_bytes(last_x.at[dt - 1], b2_r.at[dt - 1])
        lower += last_x[dt - 1].astype(jnp.float32)
    total = jnp.concatenate([upper, lower], axis=0)
    own = (x_ref[...].astype(jnp.float32) + total).astype(jnp.bfloat16)

    mids[c] = own
    send(mids.at[c], mids.at[c], mid_s, mid_r, device(1, 0, 0, 0))
    wait_bytes(mids.at[0], mid_r)

    for chunk in range(chunks):
        these = pl.ds(chunk * per * slots, per * slots)
        block = jnp.dot(place[0, these], mids[0], preferred_element_type=jnp.float32)
        block += jnp.dot(place[1, these], mids[1], preferred_element_type=jnp.float32)
        block = block.reshape(per, slots, quarter).astype(jnp.bfloat16)
        outgoing[pl.ds(chunk * per, per)] = block
        low = chunk * per
        if low == self_k:
            arrived[t, self_k] = block[0]

        def go(k, carry):
            send(
                outgoing.at[k],
                arrived.at[t, k],
                go_s.at[k],
                go_r.at[k],
                device(0, *offset(k), 0),
                keep=False,
            )
            return carry

        lax.fori_loop(low + (low == self_k), low + per, go, 0)

    for load in expert_loads:
        load.wait()

    cut = per // 2
    ways = ((right, 1), (left, tensors - 1))
    far_away = tensors // 2

    def some(chunk):
        return pl.ds(chunk * per, per)

    def half_of(chunk, way):
        return pl.ds(chunk * per + way * cut, cut)

    def back_to(k):
        dy, dz = offset(k)
        return device(0, ny - dy, nz - dz, 0)

    def share_chunk(chunk):
        def arrive(i, carry):
            k = chunk * per + i

            @pl.when(k != self_k)
            def _():
                wait_bytes(arrived.at[t, k], go_r.at[k])

            return carry

        lax.fori_loop(0, per, arrive, 0)
        held = arrived.at[t, some(chunk)]
        for way, dt in ways:
            send(held, held, x_s.at[way, chunk], x_r.at[way, chunk], device(0, 0, 0, dt), False)

    def forward_chunk(chunk):
        for way, dt in ways:
            source = lax.rem(t + tensors - dt, tensors)
            wait_bytes(arrived.at[source, some(chunk)], x_r.at[way, chunk])
            held = arrived.at[source, half_of(chunk, way)]
            send(held, held, f_s.at[way, chunk], f_r.at[way, chunk], device(0, 0, 0, dt), False)

    def compute_chunk(chunk):
        here = some(chunk)
        source = lax.rem(t + far_away, tensors)
        for way, dt in ways:
            wait_bytes(arrived.at[source, half_of(chunk, way)], f_r.at[way, chunk])
        gate_sums = jnp.zeros((per * slots, hidden_width), jnp.float32)
        upward = jnp.zeros((per * slots, hidden_width), jnp.float32)
        squares = jnp.zeros((per, slots, 1), jnp.float32)
        for q in range(tensors):
            values = arrived[q, here].astype(jnp.float32)
            squares += jnp.sum(values * values, axis=2, keepdims=True)
        inverse = lax.rsqrt(squares / full + EPSILON)
        for q in range(tensors):
            these = slice(q * quarter, (q + 1) * quarter)
            gain = gain_expert_ref[these].reshape(1, 1, quarter)
            values = arrived[q, here].astype(jnp.float32) * inverse * gain
            values = values.reshape(per * slots, quarter).astype(jnp.bfloat16)
            gate_sums += jnp.dot(values, gate[these], preferred_element_type=jnp.float32)
            upward += jnp.dot(values, up[these], preferred_element_type=jnp.float32)
        hidden = (silu(gate_sums) * upward).astype(jnp.bfloat16)
        for dt in (far_away, 1, tensors - 1, 0):
            there = lax.rem(t + dt, tensors)
            columns = pl.ds(pl.multiple_of(there * quarter, 128), quarter)
            result = jnp.dot(hidden, down[:, columns], preferred_element_type=jnp.float32)
            pieces[dt, here] = result.reshape(per, slots, quarter).astype(jnp.bfloat16)
            if dt == far_away:
                for way, near in ways:
                    send(
                        pieces.at[dt, half_of(chunk, way)],
                        through.at[way, pl.ds(chunk * cut, cut)],
                        half_s.at[way, chunk],
                        half_r.at[way, chunk],
                        device(0, 0, 0, near),
                        False,
                    )

    def relay_chunk(chunk):
        for way, dt in ways:
            came = pl.ds(chunk * cut, cut)
            wait_bytes(through.at[way, came], half_r.at[way, chunk])
            these = half_of(chunk, way)
            both = pieces[dt, these].astype(jnp.float32) + through[way, came].astype(jnp.float32)
            pieces[dt, these] = both.astype(jnp.bfloat16)
            send(
                pieces.at[dt, some(chunk)],
                beside.at[way, some(chunk)],
                side_s.at[way, chunk],
                side_r.at[way, chunk],
                device(0, 0, 0, dt),
                False,
            )

    def return_chunk(chunk):
        here = some(chunk)
        total = pieces[0, here].astype(jnp.float32)
        for way, dt in ways:
            wait_bytes(beside.at[way, here], side_r.at[way, chunk])
            total += beside[way, here].astype(jnp.float32)
        summed[here] = total.astype(jnp.bfloat16)

        def give(i, carry):
            k = chunk * per + i

            @pl.when(k != self_k)
            def _():
                send(
                    summed.at[k],
                    returned.at[k],
                    back_s.at[k],
                    back_r.at[k],
                    back_to(k),
                    False,
                )

            return carry

        lax.fori_loop(0, per, give, 0)

    work = ((0, share_chunk), (1, forward_chunk), (2, compute_chunk), (3, relay_chunk), (4, return_chunk))

    def dense_sent():
        for copy in started:
            copy.wait_send()
        for i in range(tensors - 1):
            wait_bytes(along_x.at[i], a1_s.at[i])
        for dy in range(ny - 1):
            for q in range(tensors):
                wait_bytes(along_y.at[dy, q], b1_s.at[dy, q])

        @pl.when(sends_weights)
        def _():
            for m in range(3):
                for copy in first_hop(m):
                    copy.wait_send()

    def stage(i, carry):
        for lag, act in work:

            @pl.when((i >= lag) & (i < chunks + lag))
            def _(lag=lag, act=act):
                act(i - lag)

        @pl.when(i == chunks // 2)
        def _():
            plan_routes(True)

        @pl.when(i == chunks // 2 + 1)
        def _():
            dense_sent()

        return carry

    lax.fori_loop(0, chunks + len(work) - 1, stage, 0)
    returned[self_k] = summed[self_k]

    def sent_rows(k, carry):
        wait_bytes(outgoing.at[k], go_s.at[k])
        return carry

    lax.fori_loop(0, self_k, sent_rows, 0)
    lax.fori_loop(self_k + 1, chips, sent_rows, 0)

    def sent_chunk(chunk, carry):
        for way, dt in ways:
            wait_bytes(arrived.at[0, some(chunk)], x_s.at[way, chunk])
            wait_bytes(arrived.at[0, half_of(chunk, way)], f_s.at[way, chunk])
            wait_bytes(arrived.at[0, half_of(chunk, way)], half_s.at[way, chunk])
            wait_bytes(pieces.at[0, some(chunk)], side_s.at[way, chunk])
        return carry

    lax.fori_loop(0, chunks, sent_chunk, 0)

    def arrive_back(k, carry):
        wait_bytes(returned.at[k], back_r.at[k])
        return carry

    mixed = [jnp.zeros((tokens, quarter), jnp.float32) for _ in range(2)]
    for g in range(4):
        low, high = g * chips // 4, (g + 1) * chips // 4
        lax.fori_loop(low, min(high, self_k), arrive_back, 0)
        lax.fori_loop(max(low, self_k + 1), high, arrive_back, 0)
        back = returned[low:high].reshape(all_slots // 4, quarter)
        for m in range(2):
            for j in range(2):
                mixed[m] += jnp.dot(mixers[g, m, j], back, preferred_element_type=jnp.float32)
    for m in range(2):
        mixes[0, m] = mixed[m]
    send(mixes.at[0], mixes.at[1], mix_s, mix_r, device(1, 0, 0, 0), False)
    wait_bytes(mixes.at[1], mix_r)
    for m in range(2):
        middle = mids[m]
        final = middle.astype(jnp.float32) + (mixes[0, m] + mixes[1, m])
        out_ref[m] = jnp.where(c == 0, middle, final.astype(jnp.bfloat16))

    wait_bytes(mixes.at[0], mix_s)

    def sent(k, carry):
        wait_bytes(summed.at[k], back_s.at[k])
        return carry

    lax.fori_loop(0, self_k, sent, 0)
    lax.fori_loop(self_k + 1, chips, sent, 0)


def body(
    split,
    tensors,
    activations,
    expert_ids,
    route_weights,
    gain_dense,
    gain_expert,
    dense_gate,
    dense_up,
    dense_down,
    expert_gate,
    expert_up,
    expert_down,
):
    ny, nz = split
    chips = ny * nz
    half = ny // 2
    tokens, quarter = activations.shape[1:]
    full = quarter * tensors
    rows, dense_hidden = dense_gate.shape
    width = dense_hidden // ny
    slots = 2 * CAP
    hidden = expert_gate.shape[2]
    group = ny * tensors - 1
    steps = nz // 2
    bf16, f32 = jnp.bfloat16, jnp.float32
    dma = pltpu.SemaphoreType.DMA
    vmem = pl.BlockSpec(memory_space=pltpu.VMEM)
    hbm = pl.BlockSpec(memory_space=pl.ANY)
    sent_rows = (chips, slots, quarter)
    sections = pl.pallas_call(
        functools.partial(kernel, split, tensors),
        out_shape=jax.ShapeDtypeStruct((2, tokens, quarter), bf16),
        in_specs=[hbm] + [vmem] * 4 + [hbm] * 6,
        out_specs=vmem,
        scratch_shapes=[
            pltpu.VMEM((tokens, quarter), bf16),
            pltpu.VMEM((3, rows, dense_hidden), bf16),
            pltpu.VMEM((tensors, ny, tokens, quarter), bf16),
            pltpu.VMEM((chips, 3, rows, width), bf16),
            pltpu.VMEM((ny * tokens, width), bf16),
            pltpu.VMEM((tensors, ny, tokens, quarter), bf16),
            pltpu.VMEM((tensors - 1, ny, tokens // 2, quarter), bf16),
            pltpu.VMEM((ny - 1, tensors, tokens // 2, quarter), bf16),
            pltpu.VMEM((ny, tokens // 2, quarter), bf16),
            pltpu.VMEM((tensors, tokens // 2, quarter), bf16),
            pltpu.VMEM((ny - 1, tokens // 2, quarter), bf16),
            pltpu.VMEM((tensors - 1, tokens // 2, quarter), bf16),
            pltpu.VMEM((full, hidden), bf16),
            pltpu.VMEM((full, hidden), bf16),
            pltpu.VMEM((hidden, full), bf16),
            pltpu.VMEM((2, chips * slots, tokens), bf16),
            pltpu.VMEM((4, 2, 2, tokens, chips // 4 * slots), bf16),
            pltpu.VMEM((2, tokens, quarter), bf16),
            pltpu.VMEM(sent_rows, bf16),
            pltpu.VMEM((tensors, *sent_rows), bf16),
            pltpu.VMEM((tensors, *sent_rows), bf16),
            pltpu.VMEM((2, chips // 2, slots, quarter), bf16),
            pltpu.VMEM((2, *sent_rows), bf16),
            pltpu.VMEM(sent_rows, bf16),
            pltpu.VMEM(sent_rows, bf16),
            pltpu.VMEM((2, 2, tokens, quarter), f32),
            dma((7,)),
            dma((group,)),
            dma((group,)),
            dma((ny - 1, 3)),
            dma((half, 3)),
            dma((3, 2, half, steps)),
            dma((3, 2, half, steps)),
            dma((3, half, nz)),
            dma((3, half, nz)),
            dma((tensors - 1,)),
            dma((tensors - 1,)),
            dma((ny - 1, tensors)),
            dma((ny - 1, tensors)),
            dma((ny - 1,)),
            dma((ny - 1,)),
            dma((tensors - 1,)),
            dma((tensors - 1,)),
            dma(()),
            dma(()),
            dma((chips,)),
            dma((chips,)),
            dma((2, 2 * ny)),
            dma((2, 2 * ny)),
            dma((2, 2 * ny)),
            dma((2, 2 * ny)),
            dma((2, 2 * ny)),
            dma((2, 2 * ny)),
            dma((2, 2 * ny)),
            dma((2, 2 * ny)),
            dma((chips,)),
            dma((chips,)),
            dma(()),
            dma(()),
        ],
        compiler_params=pltpu.CompilerParams(
            collective_id=0, has_side_effects=True, vmem_limit_bytes=58 * 2**20
        ),
        name="sections",
    )(
        activations[0],
        expert_ids.transpose(2, 0, 1),
        route_weights.transpose(2, 0, 1),
        gain_dense,
        gain_expert,
        dense_gate,
        dense_up,
        dense_down,
        expert_gate,
        expert_up,
        expert_down,
    )
    return sections[None]


def solution(mesh, split=SPLIT):
    placed = (
        P("segment", "expert", "tensor"),
        P(None, "expert", None),
        P(None, "expert", None),
        P(),
        P(),
        P("expert", "tensor"),
        P("expert", "tensor"),
        P("expert", "tensor"),
        P("expert", None, "tensor"),
        P("expert", None, "tensor"),
        P("expert", "tensor", None),
    )
    return jax.shard_map(
        functools.partial(body, split, mesh.shape["tensor"]),
        mesh=mesh,
        in_specs=placed,
        out_specs=P("segment", None, "expert", "tensor"),
        check_vma=False,
    )
```

```python
import functools

import jax
import jax.numpy as jnp
from jax import lax
from jax.experimental import pallas as pl
from jax.experimental.pallas import tpu as pltpu
from jax.sharding import PartitionSpec as P

EPSILON = 1e-06
MESH = pl.DeviceIdType.MESH
CAP = 12
SPLIT = (4, 8)


def wait_bytes(ref, sem):
    pltpu.make_async_copy(ref, ref, sem).wait()


def places(split, tensors):
    ny, nz = split
    c, p, t = lax.axis_index("segment"), lax.axis_index("expert"), lax.axis_index("tensor")
    y, z = p // nz, p % nz

    def device(dc=0, dy=0, dz=0, dt=0):
        return (
            lax.rem(c + dc, 2),
            lax.rem(y + dy + ny, ny) * nz + lax.rem(z + dz + nz, nz),
            lax.rem(t + dt, tensors),
        )

    return c, p, t, y, z, device


def greet(offsets, device):
    barrier = pltpu.get_barrier_semaphore()
    for offset in offsets:
        pl.semaphore_signal(barrier, inc=1, device_id=device(*offset), device_id_type=MESH)
    pl.semaphore_wait(barrier, len(offsets))


def silu(v):
    return v / (1.0 + jnp.exp(-v))


def kernel(
    split,
    tensors,
    x_hbm,
    ids_ref,
    route_ref,
    gain_dense_ref,
    gain_expert_ref,
    dense_gate_hbm,
    dense_up_hbm,
    dense_down_hbm,
    gate_hbm,
    up_hbm,
    down_hbm,
    out_ref,
    x_ref,
    dense_held,
    xbuf,
    wbuf,
    hidden_ref,
    part,
    along_x,
    along_y,
    over_x,
    over_y,
    last_y,
    last_x,
    gate,
    up,
    down,
    place,
    mixers,
    mids,
    outgoing,
    arrived,
    pieces,
    through,
    beside,
    summed,
    returned,
    mixes,
    load_sem,
    tok_s,
    tok_r,
    w1_s,
    w1_r,
    ring_s,
    ring_r,
    sib_s,
    sib_r,
    a1_s,
    a1_r,
    b1_s,
    b1_r,
    a2_s,
    a2_r,
    b2_s,
    b2_r,
    mid_s,
    mid_r,
    go_s,
    go_r,
    x_s,
    x_r,
    f_s,
    f_r,
    half_s,
    half_r,
    side_s,
    side_r,
    back_s,
    back_r,
    mix_s,
    mix_r,
):
    ny, nz = split
    chips = ny * nz
    half = ny // 2
    c, p, t, y, z, device = places(split, tensors)
    tokens, quarter = x_ref.shape
    full = quarter * tensors
    rows, width = wbuf.shape[2:]
    per_quarter = quarter // rows
    slots = 2 * CAP
    all_slots = chips * slots
    hidden_width = gate.shape[1]
    right, left = 0, 1
    signs = (1, -1)
    first, second = pl.ds(0, tokens // 2), pl.ds(tokens // 2, tokens // 2)

    dense_loads = [
        pltpu.make_async_copy(far, dense_held.at[m], load_sem.at[m])
        for m, far in enumerate((dense_gate_hbm, dense_up_hbm, dense_down_hbm))
    ]
    dense_loads.append(pltpu.make_async_copy(x_hbm, x_ref, load_sem.at[3]))
    expert_loads = [
        pltpu.make_async_copy(far.at[c], near, load_sem.at[4 + i])
        for i, (far, near) in enumerate(((gate_hbm, gate), (up_hbm, up), (down_hbm, down)))
    ]
    for load in dense_loads + expert_loads:
        load.start()

    group = [(dy, dt) for dt in range(tensors) for dy in range(ny) if dy or dt]
    offsets = {(0, dy, 0, dt) for dy, dt in group}
    offsets |= {(1, 0, 0, 0)}
    offsets |= {(0, dy, dz, 0) for dy in range(ny) for dz in range(nz) if dy or dz}
    greet(sorted(offsets), device)
    for load in dense_loads:
        load.wait()

    started = []

    def send(src, dst, send_sem, recv_sem, to, keep=True):
        copy = pltpu.make_async_remote_copy(
            src_ref=src,
            dst_ref=dst,
            send_sem=send_sem,
            recv_sem=recv_sem,
            device_id=to,
            device_id_type=MESH,
        )
        copy.start()
        if keep:
            started.append(copy)

    def first_hop(m):
        copies = []
        for dy in range(1, ny):
            there = lax.rem(y + dy, ny)
            columns = pl.ds(pl.multiple_of(there * width, 128), width)
            copies.append(
                pltpu.make_async_remote_copy(
                    src_ref=dense_held.at[m, :, columns],
                    dst_ref=wbuf.at[p, m],
                    send_sem=w1_s.at[dy - 1, m],
                    recv_sem=w1_r.at[lax.rem(y, half), m],
                    device_id=device(0, dy, 0, 0),
                    device_id_type=MESH,
                )
            )
        return copies

    sends_weights = y // half == c

    @pl.when(sends_weights)
    def _():
        for m in range(3):
            for copy in first_hop(m):
                copy.start()
            columns = pl.ds(pl.multiple_of(y * width, 128), width)
            pltpu.make_async_copy(
                dense_held.at[m, :, columns], wbuf.at[p, m], w1_r.at[lax.rem(y, half), m]
            ).start()

    hops = {}
    for a in range(half):
        far, near = nz // 2, (nz - 1) // 2
        hops[right, a], hops[left, a] = (far, near) if a % 2 == 0 else (near, far)

    def piece(core, a, dz):
        return (half * core + a) * nz + lax.rem(z + dz + nz, nz)

    def forward(kind, a, direction, step):
        sign = signs[direction]
        held = wbuf.at[piece(c, a, -sign * (step - 1)), kind]
        send(
            held,
            held,
            ring_s.at[kind, direction, a, step - 1],
            ring_r.at[kind, direction, a, step - 1],
            device(0, 0, sign % nz, 0),
        )

    def hand_over(kind, a, dz):
        held = wbuf.at[piece(c, a, dz), kind]
        send(held, held, sib_s.at[kind, a, dz % nz], sib_r.at[kind, a, dz % nz], device(1, 0, 0, 0))

    def begin(kind, a):
        wait_bytes(wbuf.at[piece(c, a, 0), kind], w1_r.at[a, kind])
        for direction in (right, left):
            if hops[direction, a] >= 1:
                forward(kind, a, direction, 1)
        hand_over(kind, a, 0)

    def ring(kind, a, step):
        for direction in (right, left):
            if step > hops[direction, a]:
                continue
            sign = signs[direction]
            wait_bytes(
                wbuf.at[piece(c, a, -sign * step), kind],
                ring_r.at[kind, direction, a, step - 1],
            )
            if step + 1 <= hops[direction, a]:
                forward(kind, a, direction, step + 1)
            hand_over(kind, a, -sign * step)

    def from_other_core(kind, a):
        for dz in range(nz):
            wait_bytes(wbuf.at[piece(1 - c, a, dz), kind], sib_r.at[kind, a, dz])

    for kind in range(2):
        for a in range(half):
            begin(kind, a)

    for i, (dy, dt) in enumerate(group):
        send(x_ref, xbuf.at[t, y], tok_s.at[i], tok_r.at[i], device(0, dy, 0, dt))
    xbuf[t, y] = x_ref[...]

    per = nz // 2
    chunks = 2 * ny
    self_k = chips - per

    def offset(k):
        chunk = k // per
        dy = (chunk // 2 + 1) % ny
        i = (chunk + chunk // (chunks - 2)) % 2 * per + k % per
        dz = i % 2 * ((i + 1) // 2) + (i + 1) % 2 * ((nz - i // 2) % nz)
        return dy, dz

    def expert_at(k):
        dy, dz = offset(k)
        there = (y + dy) % ny * nz + (z + dz) % nz
        return 2 * there + c

    def iotas(shape):
        return (lax.broadcasted_iota(jnp.int32, shape, i) for i in range(2))

    def mix_plan(m, ranks, share, chosen):
        ranks_t, share_t = ranks.T.astype(jnp.bfloat16), share.T
        high = share_t.astype(jnp.bfloat16)
        low = (share_t - high.astype(jnp.float32)).astype(jnp.bfloat16)
        for g in range(4):
            chip, slot = iotas((chips, all_slots // 4))
            spread = jnp.where(slot // slots + g * (chips // 4) == chip, 1.0, 0.0)
            spread = spread.astype(jnp.bfloat16)
            found = jnp.dot(ranks_t, spread, preferred_element_type=jnp.float32)
            token, slot = iotas((tokens, all_slots // 4))
            here = chosen(found, slot, m)
            for i, values in enumerate((high, low)):
                values = jnp.dot(values, spread, preferred_element_type=jnp.float32)
                mixers[g, m, i] = jnp.where(here, values, 0.0).astype(jnp.bfloat16)

    def plan_routes(mixing):
        experts = expert_at(lax.broadcasted_iota(jnp.int32, (chips, tokens), 0))
        one, two = iotas((tokens, tokens))
        before = jnp.where(one < two, 1.0, 0.0).astype(jnp.bfloat16)
        slot, chip = iotas((all_slots, chips))
        spread_t = jnp.where(slot // slots == chip, 1.0, 0.0).astype(jnp.bfloat16)

        def chosen(found, slot, m):
            rank = jnp.where((slot // CAP) % 2 == m, slot % CAP, 2 * tokens)
            return found == rank.astype(jnp.float32)

        for m in range(2):
            named = jnp.zeros((chips, tokens), jnp.float32)
            share = jnp.zeros((chips, tokens), jnp.float32)
            for j in range(ids_ref.shape[0]):
                same = ids_ref[j, m : m + 1, :] == experts
                named += jnp.where(same, 1.0, 0.0)
                share += jnp.where(same, route_ref[j, m : m + 1, :], 0.0)
            ranks = jnp.dot(
                named.astype(jnp.bfloat16), before, preferred_element_type=jnp.float32
            )
            ranks = jnp.where(named > 0.5, ranks, -1.0)
            if mixing:
                mix_plan(m, ranks, share, chosen)
                continue
            found = jnp.dot(
                spread_t, ranks.astype(jnp.bfloat16), preferred_element_type=jnp.float32
            )
            slot, token = iotas((all_slots, tokens))
            place[m] = jnp.where(chosen(found, slot, m), 1.0, 0.0).astype(jnp.bfloat16)

    def norm_block(j, carry):
        squares = jnp.zeros((tokens, 1), jnp.float32)
        for q in range(tensors):
            values = xbuf[q, j].astype(jnp.float32)
            squares += jnp.sum(values * values, axis=1, keepdims=True)
        inverse = lax.rsqrt(squares / full + EPSILON)
        for q in range(tensors):
            values = xbuf[q, j].astype(jnp.float32)
            gain = gain_dense_ref[q * quarter : (q + 1) * quarter].reshape(1, quarter)
            xbuf[q, j] = (values * inverse * gain).astype(jnp.bfloat16)
        return carry

    acc = [jnp.zeros((ny * tokens, width), jnp.float32) for _ in range(2)]

    def add_quarter(q):
        normed = xbuf[q].reshape(ny * tokens, quarter)
        held = pl.ds(q * per_quarter, per_quarter)
        for i in range(2):
            acc[i] += jnp.dot(
                normed, wbuf[held, i].reshape(quarter, width), preferred_element_type=jnp.float32
            )

    def give_quarter(q):
        held = wbuf[pl.ds(q * per_quarter, per_quarter), 2].reshape(quarter, width)
        result = lax.dot_general(
            hidden_ref[...], held, (((1,), (1,)), ((), ())), preferred_element_type=jnp.float32
        )
        part[q] = result.astype(jnp.bfloat16).reshape(ny, tokens, quarter)
        for dy in range(1, ny):
            send(
                part.at[q, lax.rem(y + dy, ny), second],
                along_y.at[dy - 1, q],
                b1_s.at[dy - 1, q],
                b1_r.at[dy - 1, q],
                device(0, dy, 0, 0),
                keep=False,
            )
        dt = lax.rem(q - t + tensors, tensors)

        @pl.when(dt > 0)
        def _():
            send(
                part.at[q, :, first],
                along_x.at[dt - 1],
                a1_s.at[dt - 1],
                a1_r.at[dt - 1],
                device(0, 0, 0, dt),
                keep=False,
            )

    def quarters(a):
        last = [((q + 1) * per_quarter - 1) // nz % half for q in range(tensors)]
        return [q for q in range(tensors) if last[q] == a]

    steps = nz // 2
    early = max(steps - 1, 1)
    for step in range(1, steps + 1):
        for kind in range(2):
            for a in range(half):
                ring(kind, a, step)
        if step == max(steps - 2, 1):
            begin(2, 0)
        if step == early and half > 1:
            begin(2, half - 1)
        if step == early:
            for i in range(len(group)):
                wait_bytes(xbuf.at[0, 0], tok_r.at[i])
            lax.fori_loop(0, ny, norm_block, 0)
    left_over = list(range(tensors))
    for step in range(1, steps + 1):
        ring(2, 0, step)
        if half > 1 and step < steps:
            ring(2, half - 1, step)
        if step == 1:
            for a in range(half):
                from_other_core(0, a)
                from_other_core(1, a)
        if step < steps and left_over:
            add_quarter(left_over.pop(0))
    for q in left_over:
        add_quarter(q)
    hidden_ref[...] = (silu(acc[0]) * acc[1]).astype(jnp.bfloat16)
    for a in range(half):
        if a:
            ring(2, a, steps)
        from_other_core(2, a)
        for q in quarters(a):
            give_quarter(q)
    plan_routes(False)

    total = part[t, :, first].astype(jnp.float32)
    for i in range(tensors - 1):
        wait_bytes(along_x.at[i], a1_r.at[i])
        total += along_x[i].astype(jnp.float32)
    over_x[...] = total.astype(jnp.bfloat16)
    for dy in range(1, ny):
        send(
            over_x.at[lax.rem(y + dy, ny)],
            last_y.at[dy - 1],
            a2_s.at[dy - 1],
            a2_r.at[dy - 1],
            device(0, dy, 0, 0),
        )
    total = part[:, y, second].astype(jnp.float32)
    for dy in range(1, ny):
        for q in range(tensors):
            wait_bytes(along_y.at[dy - 1, q], b1_r.at[dy - 1, q])
        total += along_y[dy - 1].astype(jnp.float32)
    over_y[...] = total.astype(jnp.bfloat16)
    for dt in range(1, tensors):
        send(
            over_y.at[lax.rem(t + dt, tensors)],
            last_x.at[dt - 1],
            b2_s.at[dt - 1],
            b2_r.at[dt - 1],
            device(0, 0, 0, dt),
        )
    upper = over_x[y].astype(jnp.float32)
    for dy in range(1, ny):
        wait_bytes(last_y.at[dy - 1], a2_r.at[dy - 1])
        upper += last_y[dy - 1].astype(jnp.float32)
    lower = over_y[t].astype(jnp.float32)
    for dt in range(1, tensors):
        wait_bytes(last_x.at[dt - 1], b2_r.at[dt - 1])
        lower += last_x[dt - 1].astype(jnp.float32)
    total = jnp.concatenate([upper, lower], axis=0)
    own = (x_ref[...].astype(jnp.float32) + total).astype(jnp.bfloat16)

    mids[c] = own
    send(mids.at[c], mids.at[c], mid_s, mid_r, device(1, 0, 0, 0))
    wait_bytes(mids.at[0], mid_r)

    for chunk in range(chunks):
        these = pl.ds(chunk * per * slots, per * slots)
        block = jnp.dot(place[0, these], mids[0], preferred_element_type=jnp.float32)
        block += jnp.dot(place[1, these], mids[1], preferred_element_type=jnp.float32)
        block = block.reshape(per, slots, quarter).astype(jnp.bfloat16)
        outgoing[pl.ds(chunk * per, per)] = block
        low = chunk * per
        if low == self_k:
            arrived[t, self_k] = block[0]

        def go(k, carry):
            send(
                outgoing.at[k],
                arrived.at[t, k],
                go_s.at[k],
                go_r.at[k],
                device(0, *offset(k), 0),
                keep=False,
            )
            return carry

        lax.fori_loop(low + (low == self_k), low + per, go, 0)

    for load in expert_loads:
        load.wait()

    cut = per // 2
    ways = ((right, 1), (left, tensors - 1))
    far_away = tensors // 2

    def some(chunk):
        return pl.ds(chunk * per, per)

    def half_of(chunk, way):
        return pl.ds(chunk * per + way * cut, cut)

    def back_to(k):
        dy, dz = offset(k)
        return device(0, ny - dy, nz - dz, 0)

    def share_chunk(chunk):
        def arrive(i, carry):
            k = chunk * per + i

            @pl.when(k != self_k)
            def _():
                wait_bytes(arrived.at[t, k], go_r.at[k])

            return carry

        lax.fori_loop(0, per, arrive, 0)
        held = arrived.at[t, some(chunk)]
        for way, dt in ways:
            send(held, held, x_s.at[way, chunk], x_r.at[way, chunk], device(0, 0, 0, dt), False)

    def forward_chunk(chunk):
        for way, dt in ways:
            source = lax.rem(t + tensors - dt, tensors)
            wait_bytes(arrived.at[source, some(chunk)], x_r.at[way, chunk])
            held = arrived.at[source, half_of(chunk, way)]
            send(held, held, f_s.at[way, chunk], f_r.at[way, chunk], device(0, 0, 0, dt), False)

    def compute_chunk(chunk):
        here = some(chunk)
        source = lax.rem(t + far_away, tensors)
        for way, dt in ways:
            wait_bytes(arrived.at[source, half_of(chunk, way)], f_r.at[way, chunk])
        gate_sums = jnp.zeros((per * slots, hidden_width), jnp.float32)
        upward = jnp.zeros((per * slots, hidden_width), jnp.float32)
        squares = jnp.zeros((per, slots, 1), jnp.float32)
        for q in range(tensors):
            values = arrived[q, here].astype(jnp.float32)
            squares += jnp.sum(values * values, axis=2, keepdims=True)
        inverse = lax.rsqrt(squares / full + EPSILON)
        for q in range(tensors):
            these = slice(q * quarter, (q + 1) * quarter)
            gain = gain_expert_ref[these].reshape(1, 1, quarter)
            values = arrived[q, here].astype(jnp.float32) * inverse * gain
            values = values.reshape(per * slots, quarter).astype(jnp.bfloat16)
            gate_sums += jnp.dot(values, gate[these], preferred_element_type=jnp.float32)
            upward += jnp.dot(values, up[these], preferred_element_type=jnp.float32)
        hidden = (silu(gate_sums) * upward).astype(jnp.bfloat16)
        for dt in (far_away, 1, tensors - 1, 0):
            there = lax.rem(t + dt, tensors)
            columns = pl.ds(pl.multiple_of(there * quarter, 128), quarter)
            result = jnp.dot(hidden, down[:, columns], preferred_element_type=jnp.float32)
            pieces[dt, here] = result.reshape(per, slots, quarter).astype(jnp.bfloat16)
            if dt == far_away:
                for way, near in ways:
                    send(
                        pieces.at[dt, half_of(chunk, way)],
                        through.at[way, pl.ds(chunk * cut, cut)],
                        half_s.at[way, chunk],
                        half_r.at[way, chunk],
                        device(0, 0, 0, near),
                        False,
                    )

    def relay_chunk(chunk):
        for way, dt in ways:
            came = pl.ds(chunk * cut, cut)
            wait_bytes(through.at[way, came], half_r.at[way, chunk])
            these = half_of(chunk, way)
            both = pieces[dt, these].astype(jnp.float32) + through[way, came].astype(jnp.float32)
            pieces[dt, these] = both.astype(jnp.bfloat16)
            send(
                pieces.at[dt, some(chunk)],
                beside.at[way, some(chunk)],
                side_s.at[way, chunk],
                side_r.at[way, chunk],
                device(0, 0, 0, dt),
                False,
            )

    def return_chunk(chunk):
        here = some(chunk)
        total = pieces[0, here].astype(jnp.float32)
        for way, dt in ways:
            wait_bytes(beside.at[way, here], side_r.at[way, chunk])
            total += beside[way, here].astype(jnp.float32)
        summed[here] = total.astype(jnp.bfloat16)

        def give(i, carry):
            k = chunk * per + i

            @pl.when(k != self_k)
            def _():
                send(
                    summed.at[k],
                    returned.at[k],
                    back_s.at[k],
                    back_r.at[k],
                    back_to(k),
                    False,
                )

            return carry

        lax.fori_loop(0, per, give, 0)

    work = ((0, share_chunk), (2, forward_chunk), (3, compute_chunk), (4, relay_chunk), (5, return_chunk))

    def dense_sent():
        for copy in started:
            copy.wait_send()
        for i in range(tensors - 1):
            wait_bytes(along_x.at[i], a1_s.at[i])
        for dy in range(ny - 1):
            for q in range(tensors):
                wait_bytes(along_y.at[dy, q], b1_s.at[dy, q])

        @pl.when(sends_weights)
        def _():
            for m in range(3):
                for copy in first_hop(m):
                    copy.wait_send()

    def stage(i, carry):
        for lag, act in work:

            @pl.when((i >= lag) & (i < chunks + lag))
            def _(lag=lag, act=act):
                act(i - lag)

        @pl.when(i == chunks // 2)
        def _():
            plan_routes(True)

        @pl.when(i == chunks // 2 + 1)
        def _():
            dense_sent()

        return carry

    lax.fori_loop(0, chunks + len(work), stage, 0)
    returned[self_k] = summed[self_k]

    def sent_rows(k, carry):
        wait_bytes(outgoing.at[k], go_s.at[k])
        return carry

    lax.fori_loop(0, self_k, sent_rows, 0)
    lax.fori_loop(self_k + 1, chips, sent_rows, 0)

    def sent_chunk(chunk, carry):
        for way, dt in ways:
            wait_bytes(arrived.at[0, some(chunk)], x_s.at[way, chunk])
            wait_bytes(arrived.at[0, half_of(chunk, way)], f_s.at[way, chunk])
            wait_bytes(arrived.at[0, half_of(chunk, way)], half_s.at[way, chunk])
            wait_bytes(pieces.at[0, some(chunk)], side_s.at[way, chunk])
        return carry

    lax.fori_loop(0, chunks, sent_chunk, 0)

    def arrive_back(k, carry):
        wait_bytes(returned.at[k], back_r.at[k])
        return carry

    mixed = [jnp.zeros((tokens, quarter), jnp.float32) for _ in range(2)]
    for g in range(4):
        low, high = g * chips // 4, (g + 1) * chips // 4
        lax.fori_loop(low, min(high, self_k), arrive_back, 0)
        lax.fori_loop(max(low, self_k + 1), high, arrive_back, 0)
        back = returned[low:high].reshape(all_slots // 4, quarter)
        for m in range(2):
            for j in range(2):
                mixed[m] += jnp.dot(mixers[g, m, j], back, preferred_element_type=jnp.float32)
    for m in range(2):
        mixes[0, m] = mixed[m]
    send(mixes.at[0], mixes.at[1], mix_s, mix_r, device(1, 0, 0, 0), False)
    wait_bytes(mixes.at[1], mix_r)
    for m in range(2):
        middle = mids[m]
        final = middle.astype(jnp.float32) + (mixes[0, m] + mixes[1, m])
        out_ref[m] = jnp.where(c == 0, middle, final.astype(jnp.bfloat16))

    wait_bytes(mixes.at[0], mix_s)

    def sent(k, carry):
        wait_bytes(summed.at[k], back_s.at[k])
        return carry

    lax.fori_loop(0, self_k, sent, 0)
    lax.fori_loop(self_k + 1, chips, sent, 0)


def body(
    split,
    tensors,
    activations,
    expert_ids,
    route_weights,
    gain_dense,
    gain_expert,
    dense_gate,
    dense_up,
    dense_down,
    expert_gate,
    expert_up,
    expert_down,
):
    ny, nz = split
    chips = ny * nz
    half = ny // 2
    tokens, quarter = activations.shape[1:]
    full = quarter * tensors
    rows, dense_hidden = dense_gate.shape
    width = dense_hidden // ny
    slots = 2 * CAP
    hidden = expert_gate.shape[2]
    group = ny * tensors - 1
    steps = nz // 2
    bf16, f32 = jnp.bfloat16, jnp.float32
    dma = pltpu.SemaphoreType.DMA
    vmem = pl.BlockSpec(memory_space=pltpu.VMEM)
    hbm = pl.BlockSpec(memory_space=pl.ANY)
    sent_rows = (chips, slots, quarter)
    sections = pl.pallas_call(
        functools.partial(kernel, split, tensors),
        out_shape=jax.ShapeDtypeStruct((2, tokens, quarter), bf16),
        in_specs=[hbm] + [vmem] * 4 + [hbm] * 6,
        out_specs=vmem,
        scratch_shapes=[
            pltpu.VMEM((tokens, quarter), bf16),
            pltpu.VMEM((3, rows, dense_hidden), bf16),
            pltpu.VMEM((tensors, ny, tokens, quarter), bf16),
            pltpu.VMEM((chips, 3, rows, width), bf16),
            pltpu.VMEM((ny * tokens, width), bf16),
            pltpu.VMEM((tensors, ny, tokens, quarter), bf16),
            pltpu.VMEM((tensors - 1, ny, tokens // 2, quarter), bf16),
            pltpu.VMEM((ny - 1, tensors, tokens // 2, quarter), bf16),
            pltpu.VMEM((ny, tokens // 2, quarter), bf16),
            pltpu.VMEM((tensors, tokens // 2, quarter), bf16),
            pltpu.VMEM((ny - 1, tokens // 2, quarter), bf16),
            pltpu.VMEM((tensors - 1, tokens // 2, quarter), bf16),
            pltpu.VMEM((full, hidden), bf16),
            pltpu.VMEM((full, hidden), bf16),
            pltpu.VMEM((hidden, full), bf16),
            pltpu.VMEM((2, chips * slots, tokens), bf16),
            pltpu.VMEM((4, 2, 2, tokens, chips // 4 * slots), bf16),
            pltpu.VMEM((2, tokens, quarter), bf16),
            pltpu.VMEM(sent_rows, bf16),
            pltpu.VMEM((tensors, *sent_rows), bf16),
            pltpu.VMEM((tensors, *sent_rows), bf16),
            pltpu.VMEM((2, chips // 2, slots, quarter), bf16),
            pltpu.VMEM((2, *sent_rows), bf16),
            pltpu.VMEM(sent_rows, bf16),
            pltpu.VMEM(sent_rows, bf16),
            pltpu.VMEM((2, 2, tokens, quarter), f32),
            dma((7,)),
            dma((group,)),
            dma((group,)),
            dma((ny - 1, 3)),
            dma((half, 3)),
            dma((3, 2, half, steps)),
            dma((3, 2, half, steps)),
            dma((3, half, nz)),
            dma((3, half, nz)),
            dma((tensors - 1,)),
            dma((tensors - 1,)),
            dma((ny - 1, tensors)),
            dma((ny - 1, tensors)),
            dma((ny - 1,)),
            dma((ny - 1,)),
            dma((tensors - 1,)),
            dma((tensors - 1,)),
            dma(()),
            dma(()),
            dma((chips,)),
            dma((chips,)),
            dma((2, 2 * ny)),
            dma((2, 2 * ny)),
            dma((2, 2 * ny)),
            dma((2, 2 * ny)),
            dma((2, 2 * ny)),
            dma((2, 2 * ny)),
            dma((2, 2 * ny)),
            dma((2, 2 * ny)),
            dma((chips,)),
            dma((chips,)),
            dma(()),
            dma(()),
        ],
        compiler_params=pltpu.CompilerParams(
            collective_id=0, has_side_effects=True, vmem_limit_bytes=58 * 2**20
        ),
        name="sections",
    )(
        activations[0],
        expert_ids.transpose(2, 0, 1),
        route_weights.transpose(2, 0, 1),
        gain_dense,
        gain_expert,
        dense_gate,
        dense_up,
        dense_down,
        expert_gate,
        expert_up,
        expert_down,
    )
    return sections[None]


def solution(mesh, split=SPLIT):
    placed = (
        P("segment", "expert", "tensor"),
        P(None, "expert", None),
        P(None, "expert", None),
        P(),
        P(),
        P("expert", "tensor"),
        P("expert", "tensor"),
        P("expert", "tensor"),
        P("expert", None, "tensor"),
        P("expert", None, "tensor"),
        P("expert", "tensor", None),
    )
    return jax.shard_map(
        functools.partial(body, split, mesh.shape["tensor"]),
        mesh=mesh,
        in_specs=placed,
        out_specs=P("segment", None, "expert", "tensor"),
        check_vma=False,
    )
```
